256 devices in a mesh: dp: 32 (over x, z_hi, core), tensor: 8 (over y, z_lo).
Axes of the slice: x: 4, y: 4, z: 8 (z_hi: 4, z_lo: 2; z = z_hi * 2 + z_lo), core: 2. Of those that a mesh axis runs over, the one named last changes fastest.
Arguments:
- tokens: bfloat16 [8192, 6144], P('dp', 'tensor'), may hold values from -6 to 6
- attended: bfloat16 [8192, 48, 128], P('dp', 'tensor'), may hold values from -6 to 6
- out_weight: bfloat16 [128, 48, 6144], P(None, 'tensor'), may hold values from -0.078125 to 0.078125
- cotangent: bfloat16 [8192, 6144], P('dp', 'tensor'), may hold values from -6 to 6
Outputs:
- mixed: bfloat16 [8192, 6144], P('dp', 'tensor')
- grad_attended: bfloat16 [8192, 48, 128], P('dp', 'tensor')
- weight_grad: float32 [128, 48, 6144], P('dp', 'tensor')
The draws below stay inside these ranges and needn't reach their ends.
All inputs are finite; a program needn't handle non-finite values.
Results may differ from the reference program's by a relative error of at most 0.018.
Values may be sent and summed in bfloat16 or wider, within the bound.
A program may use at most 256 MiB of HBM per device.

```python
import math
import jax
import jax.numpy as jnp
from jax import lax

D = 6144
HEADS = 48
HEAD_DIM = 128
TOK_DEV = 256
TOKENS = 8192
N_DP = 32
N_TENSOR = 8


def spiked(values, key, source, target, parts, factor):
    owner, partner = [(jnp.arange(values.shape[axis_at]) // (values.shape[axis_at] // parts)).reshape([-1 if axis == axis_at else 1 for axis in range(values.ndim)]) for axis_at in (source, target)]
    chosen = jax.random.permutation(key, parts)[partner]
    strong = (owner == chosen) | (owner == (partner + parts // 2) % parts)
    return jnp.where(strong, factor * values, values)


def levels(rng, shape, cuts, least, high):
    level = 1.0
    for dim, parts in cuts:
        heights = jax.random.uniform(jax.random.fold_in(jax.random.fold_in(rng, 6), dim), (parts,), jnp.float32, least / len(cuts), high / len(cuts))
        level = level * jnp.repeat(jnp.exp(heights), shape[dim] // parts).reshape((-1,) + (1,) * (len(shape) - 1 - dim))
    return level


def bell_draw(stream_key, dims, spread, most, pieces=(), kind=jnp.bfloat16):
    result = spread * jax.random.normal(stream_key, dims, jnp.float32)
    if pieces:
        result = result * levels(stream_key, dims, pieces, -0.22, 0.18)
    return jnp.clip(result, -most, most).astype(kind)


def heavy_noise(stream_key, shape, width, most, pieces, heavy, dtype=jnp.bfloat16):
    result = width * jax.random.normal(stream_key, shape, jnp.float32)
    if pieces:
        result = result * levels(stream_key, shape, pieces, -0.22, 0.18)
    return jnp.clip(spiked(result, jax.random.fold_in(stream_key, 3), *heavy), -most, most).astype(dtype)


def setup_inputs(seed: int = 0) -> dict:
    streams_of = jax.random.split(jax.random.key(seed), 5)
    tokens = bell_draw(streams_of[0], (TOKENS, D), 1.0, 6.0, ((0, 32), (1, 8)))
    attended = heavy_noise(streams_of[1], (TOKENS, HEADS, HEAD_DIM), 1.0, 6.0, ((0, 32), (1, 8)), (0, 2, 32, 2.75))
    out_weight = bell_draw(streams_of[2], (HEAD_DIM, HEADS, D), (HEADS * HEAD_DIM) ** -0.5, 0.078125, ((1, 8),))
    cotangent = bell_draw(streams_of[3], (TOKENS, D), 1.0, 6.0, ((0, 32), (1, 8)))
    return {"tokens": tokens, "attended": attended, "out_weight": out_weight, "cotangent": cotangent}


def reference(tokens, attended, out_weight, cotangent):
    per_group = HEADS // N_TENSOR
    summed = jnp.zeros((TOKENS, D), jnp.float32)
    for group in range(N_TENSOR):
        lower = group * per_group
        upper = lower + per_group
        partial_value = jnp.einsum('the,ehd->td', attended[:, lower:upper].astype(jnp.float32), out_weight[:, lower:upper].astype(jnp.float32))
        coded = lax.optimization_barrier(partial_value.astype(jnp.bfloat16))
        summed = summed + coded.astype(jnp.float32)
    mixed = (tokens.astype(jnp.float32) + summed).astype(jnp.bfloat16)
    grad_attended = jnp.einsum('td,ehd->the', cotangent.astype(jnp.float32), out_weight.astype(jnp.float32)).astype(jnp.bfloat16)
    factor = 1.0 / math.sqrt(TOKENS)
    run_inputs = attended.reshape(N_DP, TOK_DEV, HEADS, HEAD_DIM)
    run_grads = cotangent.reshape(N_DP, TOK_DEV, D)

    def add_run(total, pair):
        term = jnp.einsum('the,td->ehd', pair[0].astype(jnp.float32), pair[1].astype(jnp.float32)) * factor
        rounded = lax.optimization_barrier(term.astype(jnp.bfloat16))
        return (total + rounded.astype(jnp.float32), None)
    weight_grad, _ = lax.scan(add_run, jnp.zeros((HEAD_DIM, HEADS, D), jnp.float32), (run_inputs, run_grads))
    return (mixed, grad_attended, weight_grad)
```

```python
import functools
import math

import jax
import jax.numpy as jnp
from jax import lax
from jax.experimental import pallas as pl
from jax.experimental.pallas import tpu as pltpu
from jax.sharding import PartitionSpec as P

MESH = pl.DeviceIdType.MESH
F32 = jnp.float32
BF16 = jnp.bfloat16

Y_OFF = (0, 0, 3, 1, 3, 1, 2, 2)
Z_OFF = (0, 1, 0, 0, 1, 1, 0, 1)
ORDER = (0, 1, 2, 3, 6, 4, 5, 7)
T = 256
E = 768
H = 384


def nt(a, b):
    return lax.dot_general(a, b, (((1,), (1,)), ((), ())), preferred_element_type=F32)


def nn(a, b):
    return lax.dot_general(a, b, (((1,), (0,)), ((), ())), preferred_element_type=F32)


def kernel(
    factor,
    tok_hbm, att_hbm, w_hbm, cot_hbm,
    mixed_hbm, gatt_hbm, wg_hbm,
    tok, a_own, a_oth, perm, at_own, at_oth, w, cot, cotx, part,
    br, bfin, bz, gacc, gout,
    term, xr, xfin, xs, zr, zfin, res, resx,
    lsem, osem, ssem, rsem,
):
    dp, tp = lax.axis_index("dp"), lax.axis_index("tensor")
    x, zh, c = dp // 8, (dp // 2) % 4, dp % 2
    y, zl = tp // 2, tp % 2

    def dev(x_, zh_, c_, y_, zl_):
        return ((x_ * 4 + zh_) * 2 + c_, y_ * 2 + zl_)

    xp, xm = dev((x + 1) % 4, zh, c, y, zl), dev((x + 3) % 4, zh, c, y, zl)
    yp, ym = dev(x, zh, c, (y + 1) % 4, zl), dev(x, zh, c, (y + 3) % 4, zl)
    zp, zm = dev(x, (zh + 1) % 4, c, y, zl), dev(x, (zh + 3) % 4, c, y, zl)
    zo, co = dev(x, zh, c, y, 1 - zl), dev(x, zh, 1 - c, y, zl)

    barrier = pltpu.get_barrier_semaphore()
    for to in (xp, xm, yp, ym, zp, zm, zo, co):
        pl.semaphore_signal(barrier, inc=1, device_id=to, device_id_type=MESH)

    def block(s):
        return ((y + Y_OFF[s]) % 4) * 2 + (zl + Z_OFF[s]) % 2

    count = [0]

    def load(src, dst):
        copy = pltpu.make_async_copy(src, dst, lsem.at[count[0]])
        count[0] += 1
        copy.start()
        return copy

    l_cot = [load(cot_hbm.at[:, pl.ds(H * h, H)], cot.at[0, h]) for h in range(2)]
    l_att = [load(att_hbm.at[h], a_own.at[:, pl.ds(128 * h, 128)]) for h in range(6)]
    l_w = {}
    for s in (7, 5, 4, 1, 6, 3, 2, 0):
        for h in range(2):
            col = pl.multiple_of(block(s) * E + H * h, 128)
            l_w[s, h] = load(w_hbm.at[:, pl.ds(col, H)], w.at[s, h])
    l_tok = load(tok_hbm, tok)

    sent = []

    def send(src, dst, to):
        i = len(sent)
        copy = pltpu.make_async_remote_copy(
            src_ref=src, dst_ref=dst, send_sem=ssem.at[i], recv_sem=rsem.at[i],
            device_id=to, device_id_type=MESH,
        )
        copy.start()
        sent.append(copy)
        return copy

    outs = []

    def store(src, dst):
        copy = pltpu.make_async_copy(src, dst, osem.at[len(outs)])
        copy.start()
        outs.append(copy)

    def make_perm(i, _):
        row = lax.broadcasted_iota(jnp.int32, (48, E), 0)
        col = lax.broadcasted_iota(jnp.int32, (48, E), 1)
        core = (row >= 24).astype(jnp.int32)
        r = row - 24 * core
        want = (r >> 2) * 128 + 8 * i + 4 * core + (r & 3)
        perm[i // 4, pl.ds(pl.multiple_of((i % 4) * 48, 16), 48), :] = (
            (col == want).astype(F32).astype(BF16)
        )
        return 0

    def permute(src, dst):
        def go(i, _):
            dst[i] = nt(perm[i], src[...]).astype(BF16)
            return 0

        lax.fori_loop(0, 4, go, 0)

    a = {}
    cx = {}

    def core_send(s):
        cx[s] = send(cot.at[s, 1 - c], cotx.at[s], co)

    pl.semaphore_wait(barrier, 8)
    for h in range(2):
        l_cot[h].wait()
    a[2, 0] = send(cot.at[0, 0], cot.at[2, 0], yp)
    a[3, 1] = send(cot.at[0, 1], cot.at[3, 1], ym)
    a[1, 0] = send(cot.at[0, 0], cot.at[1, 0], zo)
    core_send(0)
    a[2, 1] = send(cot.at[0, 1], cot.at[2, 1], yp)
    a[3, 0] = send(cot.at[0, 0], cot.at[3, 0], ym)
    a[1, 1] = send(cot.at[0, 1], cot.at[1, 1], zo)
    for cp in l_att:
        cp.wait()
    a_swap = send(a_own, a_oth, co)
    lax.fori_loop(0, 16, make_perm, 0)
    permute(a_own, at_own)
    a_swap.wait_recv()
    permute(a_oth, at_oth)

    x1, x2, z1, z2, r1 = {}, {}, {}, {}, {}

    def c_term(s):
        cx[s].wait_recv()

        def go(i, _):
            val = nn(at_own[i], cot[s, c]) + nn(at_oth[i], cotx[s])
            term[s, i] = val.astype(BF16).reshape(4, 48, H)
            return 0

        lax.fori_loop(0, 4, go, 0)
        xf, xn, xl = (x + 2) % 4, (x + 1) % 4, (x + 3) % 4
        x1[s] = [
            send(term.at[s, xf, pl.ds(0, 2)], xr.at[s, 0], xp),
            send(term.at[s, xf, pl.ds(2, 2)], xr.at[s, 1], xm),
            send(term.at[s, xn, pl.ds(2, 2)], xfin.at[s, 0, pl.ds(2, 2)], xp),
            send(term.at[s, xl, pl.ds(0, 2)], xfin.at[s, 1, pl.ds(0, 2)], xm),
        ]

    def c_relay(s):
        xn, xl = (x + 1) % 4, (x + 3) % 4
        x2[s] = []
        x1[s][0].wait_recv()
        t = term[s, xn, pl.ds(0, 2)].astype(F32) + xr[s, 0].astype(F32)
        term[s, xn, pl.ds(0, 2)] = t.astype(BF16)
        x2[s].append(send(term.at[s, xn, pl.ds(0, 2)], xfin.at[s, 0, pl.ds(0, 2)], xp))
        x1[s][1].wait_recv()
        t = term[s, xl, pl.ds(2, 2)].astype(F32) + xr[s, 1].astype(F32)
        term[s, xl, pl.ds(2, 2)] = t.astype(BF16)
        x2[s].append(send(term.at[s, xl, pl.ds(2, 2)], xfin.at[s, 1, pl.ds(2, 2)], xm))

    def z_places(s):
        even = ORDER.index(s) % 2 == 0
        up, down = (zh + 1) % 4, (zh + 3) % 4
        return (up, down, zp, zm) if even else (down, up, zm, zp)

    def c_xsum(s):
        x1[s][2].wait_recv()
        x1[s][3].wait_recv()
        x2[s][0].wait_recv()
        x2[s][1].wait_recv()
        t = term[s, x].astype(F32) + xfin[s, 0].astype(F32) + xfin[s, 1].astype(F32)
        xs[s] = t.astype(BF16)
        _, n_m, to_p, to_m = z_places(s)
        z1[s] = [
            send(xs.at[s, (zh + 2) % 4], zr.at[s], to_p),
            send(xs.at[s, n_m], zfin.at[s, 1], to_m),
        ]

    def c_zrelay(s):
        n_p, _, to_p, _ = z_places(s)
        z1[s][0].wait_recv()
        t = xs[s, n_p].astype(F32) + zr[s].astype(F32)
        xs[s, n_p] = t.astype(BF16)
        z2[s] = send(xs.at[s, n_p], zfin.at[s, 0], to_p)

    def c_zsum(s):
        z1[s][1].wait_recv()
        z2[s].wait_recv()
        t = xs[s, zh].astype(F32) + zfin[s, 0].astype(F32) + zfin[s, 1].astype(F32)
        res[s] = (t * factor).reshape(2, 24, H)
        r1[s] = send(res.at[s, 1 - c], resx.at[s], co)
        col = pl.multiple_of(block(s) * E + H * c, 128)
        store(res.at[s, c], wg_hbm.at[:, pl.ds(col, H)])

    def c_out(s):
        r1[s].wait_recv()
        col = pl.multiple_of(block(s) * E + H * (1 - c), 128)
        store(resx.at[s], wg_hbm.at[:, pl.ds(col, H)])

    def grad(s):
        def go(h, _):
            gacc[...] += nt(cot[s, h], w[s, h])
            return 0

        lax.fori_loop(0, 2, go, 0)

    def b_part(s):
        for h in range(2):
            l_w[s, h].wait()

        def go(h, _):
            part[s, h] = nn(a_own[...], w[s, h]).astype(BF16)
            return 0

        lax.fori_loop(0, 2, go, 0)

    ROUND = ((7, 5, 4, 1), (6, 3, 2, 0))
    b1, b2, b3 = {}, {}, {}

    def b_send(r):
        f, n, m, _ = ROUND[r]
        b1[r] = [
            send(part.at[f, 0], br.at[r, 0], yp),
            send(part.at[f, 1], br.at[r, 1], ym),
            send(part.at[n, 1], bfin.at[r, 0, 1], yp),
            send(part.at[m, 0], bfin.at[r, 1, 0], ym),
        ]

    def b_relay(r):
        _, n, m, _ = ROUND[r]
        b1[r][0].wait_recv()
        part[n, 0] = (part[n, 0].astype(F32) + br[r, 0].astype(F32)).astype(BF16)
        b2[r] = [send(part.at[n, 0], bfin.at[r, 0, 0], yp)]
        b1[r][1].wait_recv()
        part[m, 1] = (part[m, 1].astype(F32) + br[r, 1].astype(F32)).astype(BF16)
        b2[r].append(send(part.at[m, 1], bfin.at[r, 1, 1], ym))

    def b_sum(r, h):
        o = ROUND[r][3]
        return part[o, h].astype(F32) + bfin[r, 0, h].astype(F32) + bfin[r, 1, h].astype(F32)

    def b_wait(r):
        b1[r][2].wait_recv()
        b1[r][3].wait_recv()
        b2[r][0].wait_recv()
        b2[r][1].wait_recv()

    def b_cross():
        b_wait(0)
        for h in range(2):
            part[1, h] = b_sum(0, h).astype(BF16)
            b3[h] = send(part.at[1, h], bz.at[h], zo)

    def b_mix():
        b_wait(1)
        l_tok.wait()
        for h in range(2):
            b3[h].wait_recv()
            t = b_sum(1, h) + bz[h].astype(F32)
            tok[:, pl.ds(H * h, H)] = (tok[:, pl.ds(H * h, H)].astype(F32) + t).astype(BF16)
        store(tok, mixed_hbm)

    gacc[...] = jnp.zeros_like(gacc)
    c_term(0)
    a[2, 0].wait_recv()
    a[6, 0] = send(cot.at[2, 0], cot.at[6, 0], yp)
    a[3, 1].wait_recv()
    a[6, 1] = send(cot.at[3, 1], cot.at[6, 1], ym)
    c_relay(0)
    b_part(7)
    b_part(5)
    b_part(4)
    a[1, 0].wait_recv()
    a[1, 1].wait_recv()
    a[4, 0] = send(cot.at[1, 0], cot.at[4, 0], yp)
    a[5, 1] = send(cot.at[1, 1], cot.at[5, 1], ym)
    a[4, 1] = send(cot.at[1, 1], cot.at[4, 1], yp)
    a[5, 0] = send(cot.at[1, 0], cot.at[5, 0], ym)
    core_send(1)
    a[2, 1].wait_recv()
    core_send(2)
    a[3, 0].wait_recv()
    core_send(3)
    c_term(1)
    c_xsum(0)
    c_term(2)
    c_relay(1)
    c_zrelay(0)
    a[6, 0].wait_recv()
    a[6, 1].wait_recv()
    a[7, 0] = send(cot.at[6, 0], cot.at[7, 0], zo)
    a[7, 1] = send(cot.at[6, 1], cot.at[7, 1], zo)
    core_send(6)
    b_send(0)
    c_term(3)
    c_relay(2)
    c_xsum(1)
    c_zsum(0)
    b_part(1)
    b_part(6)
    b_part(3)
    b_part(2)
    b_part(0)
    c_term(6)
    c_relay(3)
    c_xsum(2)
    c_zrelay(1)
    for s in (0, 1, 2, 3, 6):
        grad(s)
    for s in (4, 5):
        a[s, 0].wait_recv()
        a[s, 1].wait_recv()
        core_send(s)
    c_term(4)
    c_relay(6)
    c_xsum(3)
    c_zrelay(2)
    c_zsum(1)
    b_relay(0)
    b_send(1)
    c_term(5)
    c_relay(4)
    c_xsum(6)
    c_zrelay(3)
    c_zsum(2)
    a[7, 0].wait_recv()
    a[7, 1].wait_recv()
    core_send(7)
    c_term(7)
    c_relay(5)
    c_xsum(4)
    c_zrelay(6)
    c_zsum(3)
    b_cross()
    c_relay(7)
    c_xsum(5)
    c_zrelay(4)
    c_zsum(6)
    b_relay(1)
    for s in (4, 5, 7):
        grad(s)
    for h in range(6):
        gout[h] = gacc[:, pl.ds(128 * h, 128)].astype(BF16)
    store(gout, gatt_hbm)
    c_xsum(7)
    c_zrelay(5)
    c_zsum(4)
    c_zrelay(7)
    c_zsum(5)
    for s in (0, 1, 2, 3, 6, 4):
        c_out(s)
    b_mix()
    c_zsum(7)
    c_out(5)
    c_out(7)
    for cp in sent:
        cp.wait_send()
    for cp in outs:
        cp.wait()


N_SEND = 128


def body(tokens, attended, out_weight, cotangent):
    factor = 1.0 / math.sqrt(attended.shape[0] * lax.axis_size("dp"))
    any_spec = pl.BlockSpec(memory_space=pl.ANY)
    vm = pltpu.VMEM
    mixed, gatt, wg = pl.pallas_call(
        functools.partial(kernel, factor),
        out_shape=(
            jax.ShapeDtypeStruct((T, E), BF16),
            jax.ShapeDtypeStruct((6, T, 128), BF16),
            jax.ShapeDtypeStruct((24, 8 * E), F32),
        ),
        in_specs=[any_spec] * 4,
        out_specs=(any_spec,) * 3,
        scratch_shapes=[
            vm((T, E), BF16),
            vm((T, E), BF16),
            vm((T, E), BF16),
            vm((4, 192, E), BF16),
            vm((4, 192, T), BF16),
            vm((4, 192, T), BF16),
            vm((8, 2, E, H), BF16),
            vm((8, 2, T, H), BF16),
            vm((8, T, H), BF16),
            vm((8, 2, T, H), BF16),
            vm((2, 2, T, H), BF16),
            vm((2, 2, 2, T, H), BF16),
            vm((2, T, H), BF16),
            vm((T, E), F32),
            vm((6, T, 128), BF16),
            vm((8, 4, 4, 48, H), BF16),
            vm((8, 2, 2, 48, H), BF16),
            vm((8, 2, 4, 48, H), BF16),
            vm((8, 4, 48, H), BF16),
            vm((8, 48, H), BF16),
            vm((8, 2, 48, H), BF16),
            vm((8, 2, 24, H), F32),
            vm((8, 24, H), F32),
            pltpu.SemaphoreType.DMA((25,)),
            pltpu.SemaphoreType.DMA((18,)),
            pltpu.SemaphoreType.DMA((N_SEND,)),
            pltpu.SemaphoreType.DMA((N_SEND,)),
        ],
        compiler_params=pltpu.CompilerParams(
            collective_id=0, has_side_effects=True, vmem_limit_bytes=56 * 2**20
        ),
    )(
        tokens,
        jnp.transpose(attended, (1, 0, 2)),
        jnp.transpose(out_weight, (1, 0, 2)).reshape(E, 8 * E),
        cotangent,
    )
    return (
        mixed,
        jnp.transpose(gatt, (1, 0, 2)),
        jnp.transpose(wg.reshape(6, 4, 8 * E), (1, 0, 2)),
    )


def solution(mesh):
    placed = (
        P("dp", "tensor"),
        P("dp", "tensor", None),
        P(None, "tensor", None),
        P("dp", "tensor"),
    )
    return jax.shard_map(
        body,
        mesh=mesh,
        in_specs=placed,
        out_specs=(P("dp", "tensor"), P("dp", "tensor", None), P("dp", "tensor", None)),
        check_vma=False,
    )
```

```python
import functools
import math

import jax
import jax.numpy as jnp
from jax import lax
from jax.experimental import pallas as pl
from jax.experimental.pallas import tpu as pltpu
from jax.sharding import PartitionSpec as P

MESH = pl.DeviceIdType.MESH
F32 = jnp.float32
BF16 = jnp.bfloat16

Y_OFF = (0, 0, 3, 1, 3, 1, 2, 2)
Z_OFF = (0, 1, 0, 0, 1, 1, 0, 1)
T = 256
E = 768
H = 384
DIRECT = ()


def nt(a, b):
    return lax.dot_general(a, b, (((1,), (1,)), ((), ())), preferred_element_type=F32)


def nn(a, b):
    return lax.dot_general(a, b, (((1,), (0,)), ((), ())), preferred_element_type=F32)


def kernel(
    factor,
    tok_hbm, att_hbm, w_hbm, cot_hbm,
    mixed, gatt, wg,
    tok, a_own, perm, at, w, cot, part,
    br, bfin, bz, gacc,
    term, xr, xfin, xs, zr, zfin, res, resx,
    lsem, ssem, rsem,
):
    dp, tp = lax.axis_index("dp"), lax.axis_index("tensor")
    x, zh, c = dp // 8, (dp // 2) % 4, dp % 2
    y, zl = tp // 2, tp % 2

    def dev(x_, zh_, c_, y_, zl_):
        return ((x_ * 4 + zh_) * 2 + c_, y_ * 2 + zl_)

    xp, xm = dev((x + 1) % 4, zh, c, y, zl), dev((x + 3) % 4, zh, c, y, zl)
    yp, ym = dev(x, zh, c, (y + 1) % 4, zl), dev(x, zh, c, (y + 3) % 4, zl)
    zp, zm = dev(x, (zh + 1) % 4, c, y, zl), dev(x, (zh + 3) % 4, c, y, zl)
    z2 = dev(x, (zh + 2) % 4, c, y, zl)
    zo, co = dev(x, zh, c, y, 1 - zl), dev(x, zh, 1 - c, y, zl)

    barrier = pltpu.get_barrier_semaphore()
    for to in (xp, xm, yp, ym, zp, zm, z2, zo, co):
        pl.semaphore_signal(barrier, inc=1, device_id=to, device_id_type=MESH)

    def slot(i, k):
        return (0, 2 + k, 3 - k, 1, 6, 7, 4 + k, 5 - k)[i]

    def block(s):
        return ((y + Y_OFF[s]) % 4) * 2 + (zl + Z_OFF[s]) % 2

    def step_block(i, k):
        yo = (0, 3 - 2 * k, 1 + 2 * k, 0, 2, 2, 3 - 2 * k, 1 + 2 * k)[i]
        return ((y + yo) % 4) * 2 + (zl + (0, 0, 0, 1, 0, 1, 1, 1)[i]) % 2

    count = [0]

    def load(src, dst):
        copy = pltpu.make_async_copy(src, dst, lsem.at[count[0]])
        count[0] += 1
        copy.start()
        return copy

    l_cot = [load(cot_hbm.at[:, pl.ds(H * h, H)], cot.at[0, 1 + h]) for h in range(2)]
    l_att = [load(att_hbm.at[h], a_own.at[:, pl.ds(128 * h, 128)]) for h in range(6)]
    l_w = {}
    for s in (7, 5, 4, 1, 6, 3, 2, 0):
        for h in range(2):
            col = pl.multiple_of(block(s) * E + H * h, 128)
            l_w[s, h] = load(w_hbm.at[:, pl.ds(col, H)], w.at[s, h])
    l_tok = load(tok_hbm, tok)

    sent = []

    def send(src, dst, to):
        i = len(sent)
        copy = pltpu.make_async_remote_copy(
            src_ref=src, dst_ref=dst, send_sem=ssem.at[i], recv_sem=rsem.at[i],
            device_id=to, device_id_type=MESH,
        )
        copy.start()
        sent.append(copy)
        return copy

    a, cx = {}, {}

    def a_send(src, s, h, to):
        a[s, h] = send(cot.at[src, 1 + h], cot.at[s, 1 + h], to)

    def core_send(i):
        s = slot(i, 1 - c)
        cx[i] = send(cot.at[s, 2 - c], cot.at[s, 3 * (1 - c)], co)

    def make_perm(i, _):
        row = lax.broadcasted_iota(jnp.int32, (48, 128), 0)
        core = (row >= 24).astype(jnp.int32)
        r = row - 24 * core
        want = (r >> 2) * 128 + 8 * i + 4 * core + (r & 3)
        want = want - lax.broadcasted_iota(jnp.int32, (48, 128), 1)
        rows = pl.ds(pl.multiple_of((i % 8) * 48, 16), 48)
        for h in range(6):
            perm[i // 8, rows, pl.ds(128 * h, 128)] = (
                jnp.where(want == 128 * h, 1.0, 0.0).astype(BF16)
            )
        return 0

    lax.fori_loop(0, 16, make_perm, 0)
    pl.semaphore_wait(barrier, 9)
    l_cot[0].wait()
    l_cot[1].wait()
    a_send(0, 2, 0, yp)
    a_send(0, 3, 1, ym)
    a_send(0, 1, 0, zo)
    core_send(0)
    a_send(0, 2, 1, yp)
    a_send(0, 3, 0, ym)
    a_send(0, 1, 1, zo)
    for cp in l_att:
        cp.wait()
    mine = pl.ds(pl.multiple_of(T * (1 - c), T), T)

    def permute(i, _):
        at[i, :, mine] = nt(perm[i], a_own[...]).astype(BF16)
        return 0

    lax.fori_loop(0, 2, permute, 0)
    a_swap = send(at.at[:, :, mine], at.at[:, :, mine], co)

    x1, x2, zs, zt, r1 = {}, {}, {}, {}, {}

    def c_term(i):
        cx[i].wait_recv()
        s = slot(i, c)

        val = nn(at[...].reshape(E, 2 * T), cot[s, pl.ds(2 * c, 2)].reshape(2 * T, H))
        term[i] = val.astype(BF16).reshape(4, 4, 48, H)
        xf, xn, xl = (x + 2) % 4, (x + 1) % 4, (x + 3) % 4
        x1[i] = [
            send(term.at[i, xf, pl.ds(0, 2)], xr.at[i, 0], xp),
            send(term.at[i, xf, pl.ds(2, 2)], xr.at[i, 1], xm),
            send(term.at[i, xn, pl.ds(2, 2)], xfin.at[i, 0, pl.ds(2, 2)], xp),
            send(term.at[i, xl, pl.ds(0, 2)], xfin.at[i, 1, pl.ds(0, 2)], xm),
        ]

    def c_relay(i):
        xn, xl = (x + 1) % 4, (x + 3) % 4
        x2[i] = []
        x1[i][0].wait_recv()
        t = term[i, xn, pl.ds(0, 2)].astype(F32) + xr[i, 0].astype(F32)
        term[i, xn, pl.ds(0, 2)] = t.astype(BF16)
        x2[i].append(send(term.at[i, xn, pl.ds(0, 2)], xfin.at[i, 0, pl.ds(0, 2)], xp))
        x1[i][1].wait_recv()
        t = term[i, xl, pl.ds(2, 2)].astype(F32) + xr[i, 1].astype(F32)
        term[i, xl, pl.ds(2, 2)] = t.astype(BF16)
        x2[i].append(send(term.at[i, xl, pl.ds(2, 2)], xfin.at[i, 1, pl.ds(2, 2)], xm))

    def z_places(i):
        up, down = (zh + 1) % 4, (zh + 3) % 4
        return (up, down, zp, zm) if i % 2 == 0 else (down, up, zm, zp)

    def c_xsum(i):
        x1[i][2].wait_recv()
        x1[i][3].wait_recv()
        x2[i][0].wait_recv()
        x2[i][1].wait_recv()
        t = term[i, x].astype(F32) + xfin[i, 0].astype(F32) + xfin[i, 1].astype(F32)
        xs[i] = t.astype(BF16)
        n_p, n_m, to_p, to_m = z_places(i)
        if i in DIRECT:
            zs[i] = send(xs.at[i, (zh + 2) % 4], zr.at[i], z2)
            zt[i] = send(xs.at[i, n_p], zfin.at[i, 0], to_p)
        else:
            zs[i] = send(xs.at[i, (zh + 2) % 4], zr.at[i], to_p)
        zs[i] = zs[i], send(xs.at[i, n_m], zfin.at[i, 1], to_m)

    def c_zrelay(i):
        n_p, _, to_p, _ = z_places(i)
        zs[i][0].wait_recv()
        t = xs[i, n_p].astype(F32) + zr[i].astype(F32)
        xs[i, n_p] = t.astype(BF16)
        zt[i] = send(xs.at[i, n_p], zfin.at[i, 0], to_p)

    def put(val, col):
        cols = pl.ds(pl.multiple_of(col, 128), H)
        for h in range(6):
            wg[h, :, cols] = val[4 * h : 4 * h + 4]

    def c_zsum(i):
        zs[i][1].wait_recv()
        zt[i].wait_recv()
        t = xs[i, zh].astype(F32) + zfin[i, 0].astype(F32) + zfin[i, 1].astype(F32)
        if i in DIRECT:
            zs[i][0].wait_recv()
            t = t + zr[i].astype(F32)
        res[i] = (t * factor).reshape(2, 24, H)
        r1[i] = send(res.at[i, 1 - c], resx.at[i], co)
        put(res[i, c], step_block(i, c) * E + H * c)

    def c_out(i):
        r1[i].wait_recv()
        put(resx[i], step_block(i, 1 - c) * E + H * (1 - c))

    def grad(s):
        def go(b, _):
            cols = pl.ds(pl.multiple_of(b * T, T), T)
            t = nt(cot[s, 1], w[s, 0, cols]) + nt(cot[s, 2], w[s, 1, cols])
            gacc[:, cols] += t
            return 0

        lax.fori_loop(0, 3, go, 0)

    def b_part(s):
        for h in range(2):
            l_w[s, h].wait()

        def go(h, _):
            part[s, h] = nn(a_own[...], w[s, h]).astype(BF16)
            return 0

        lax.fori_loop(0, 2, go, 0)

    ROUND = ((7, 5, 4, 1), (6, 3, 2, 0))
    b1, bn, b2, b3 = {}, {}, {}, {}

    def b_far(r):
        f = ROUND[r][0]
        b1[r] = [
            send(part.at[f, 0], br.at[r, 0], yp),
            send(part.at[f, 1], br.at[r, 1], ym),
        ]

    def b_near(r):
        _, n, m, _ = ROUND[r]
        bn[r] = [
            send(part.at[n, 1], bfin.at[r, 0, 1], yp),
            send(part.at[m, 0], bfin.at[r, 1, 0], ym),
        ]

    def b_relay(r):
        _, n, m, _ = ROUND[r]
        b1[r][0].wait_recv()
        part[n, 0] = (part[n, 0].astype(F32) + br[r, 0].astype(F32)).astype(BF16)
        b2[r] = [send(part.at[n, 0], bfin.at[r, 0, 0], yp)]
        b1[r][1].wait_recv()
        part[m, 1] = (part[m, 1].astype(F32) + br[r, 1].astype(F32)).astype(BF16)
        b2[r].append(send(part.at[m, 1], bfin.at[r, 1, 1], ym))

    def b_sum(r, h):
        o = ROUND[r][3]
        return part[o, h].astype(F32) + bfin[r, 0, h].astype(F32) + bfin[r, 1, h].astype(F32)

    def b_wait(r):
        bn[r][0].wait_recv()
        bn[r][1].wait_recv()
        b2[r][0].wait_recv()
        b2[r][1].wait_recv()

    def b_cross():
        b_wait(0)
        for h in range(2):
            part[1, h] = b_sum(0, h).astype(BF16)
            b3[h] = send(part.at[1, h], bz.at[h], zo)

    def b_mix():
        b_wait(1)
        l_tok.wait()
        for h in range(2):
            b3[h].wait_recv()
            t = b_sum(1, h) + bz[h].astype(F32)
            cols = pl.ds(H * h, H)
            mixed[:, cols] = (tok[:, cols].astype(F32) + t).astype(BF16)

    def grad_out():
        for h in range(6):
            gatt[h] = gacc[:, pl.ds(128 * h, 128)].astype(BF16)

    def arrived(*keys):
        for k in keys:
            a[k].wait_recv()

    a_swap.wait_recv()
    gacc[...] = jnp.zeros_like(gacc)
    b_part(7)
    c_term(0)
    arrived((2, 0), (3, 1))
    a_send(2, 6, 0, yp)
    a_send(3, 6, 1, ym)
    core_send(1)
    b_part(5)
    c_relay(0)
    c_term(1)
    arrived((1, 0), (1, 1))
    core_send(3)
    a_send(1, 4, 0, yp)
    a_send(1, 5, 1, ym)
    b_part(4)
    b_near(0)
    c_term(3)
    c_xsum(0)
    arrived((6, 0), (6, 1))
    a_send(6, 7, 0, zo)
    a_send(6, 7, 1, zo)
    core_send(4)
    b_part(2)
    b_part(0)
    arrived((2, 1), (3, 0))
    core_send(2)
    c_relay(3)
    c_term(4)
    c_zrelay(0)
    c_term(2)
    b_part(3)
    b_far(0)
    a_send(1, 4, 1, yp)
    a_send(1, 5, 0, ym)
    grad(0)
    c_relay(1)
    c_relay(4)
    c_xsum(3)
    arrived((4, 0), (5, 1))
    core_send(6)
    b_part(1)
    c_relay(2)
    c_term(6)
    b_relay(0)
    c_zrelay(3)
    arrived((7, 0), (7, 1))
    core_send(5)
    b_part(6)
    c_xsum(1)
    c_zsum(0)
    c_xsum(4)
    c_out(0)
    b_far(1)
    arrived((4, 1), (5, 0))
    core_send(7)
    c_term(5)
    c_xsum(2)
    c_term(7)
    c_zrelay(4)
    c_zrelay(1)
    b_cross()
    c_zsum(3)
    b_near(1)
    grad(3)
    grad(1)
    c_relay(5)
    c_relay(7)
    b_relay(1)
    grad(5)
    c_zrelay(2)
    grad(6)
    c_relay(6)
    grad(2)
    c_xsum(7)
    c_xsum(5)
    grad(7)
    c_xsum(6)
    c_zsum(1)
    grad(4)
    c_out(1)
    c_zrelay(7)
    b_mix()
    c_zrelay(5)
    c_zsum(2)
    c_zrelay(6)
    c_zsum(4)
    c_zsum(7)
    c_out(2)
    c_out(3)
    c_out(4)
    grad_out()
    c_zsum(5)
    c_zsum(6)
    c_out(7)
    c_out(5)
    c_out(6)
    for cp in sent:
        cp.wait_send()


N_SEND = 120


def body(tokens, attended, out_weight, cotangent):
    factor = 1.0 / math.sqrt(attended.shape[0] * lax.axis_size("dp"))
    any_spec = pl.BlockSpec(memory_space=pl.ANY)
    vm = pltpu.VMEM
    mixed, gatt, wg = pl.pallas_call(
        functools.partial(kernel, factor),
        out_shape=(
            vm((T, E), BF16),
            vm((6, T, 128), BF16),
            vm((6, 4, 8 * E), F32),
        ),
        in_specs=[any_spec] * 4,
        out_specs=(pl.BlockSpec(memory_space=vm),) * 3,
        scratch_shapes=[
            vm((T, E), BF16),
            vm((T, E), BF16),
            vm((2, H, E), BF16),
            vm((2, H, 2 * T), BF16),
            vm((8, 2, E, H), BF16),
            vm((8, 4, T, H), BF16),
            vm((8, 2, T, H), BF16),
            vm((2, 2, T, H), BF16),
            vm((2, 2, 2, T, H), BF16),
            vm((2, T, H), BF16),
            vm((T, E), F32),
            vm((8, 4, 4, 48, H), BF16),
            vm((8, 2, 2, 48, H), BF16),
            vm((8, 2, 4, 48, H), BF16),
            vm((8, 4, 48, H), BF16),
            vm((8, 48, H), BF16),
            vm((8, 2, 48, H), BF16),
            vm((8, 2, 24, H), F32),
            vm((8, 24, H), F32),
            pltpu.SemaphoreType.DMA((25,)),
            pltpu.SemaphoreType.DMA((N_SEND,)),
            pltpu.SemaphoreType.DMA((N_SEND,)),
        ],
        compiler_params=pltpu.CompilerParams(
            collective_id=0, has_side_effects=True, vmem_limit_bytes=56 * 2**20
        ),
    )(
        tokens,
        jnp.transpose(attended, (1, 0, 2)),
        jnp.transpose(out_weight, (1, 0, 2)).reshape(E, 8 * E),
        cotangent,
    )
    return (
        mixed,
        jnp.transpose(gatt, (1, 0, 2)),
        jnp.transpose(wg, (1, 0, 2)),
    )


def solution(mesh):
    placed = (
        P("dp", "tensor"),
        P("dp", "tensor", None),
        P(None, "tensor", None),
        P("dp", "tensor"),
    )
    return jax.shard_map(
        body,
        mesh=mesh,
        in_specs=placed,
        out_specs=(P("dp", "tensor"), P("dp", "tensor", None), P("dp", "tensor", None)),
        check_vma=False,
    )
```

```python
import functools
import math

import jax
import jax.numpy as jnp
from jax import lax
from jax.experimental import pallas as pl
from jax.experimental.pallas import tpu as pltpu
from jax.sharding import PartitionSpec as P

MESH = pl.DeviceIdType.MESH
F32 = jnp.float32
BF16 = jnp.bfloat16

Y_OFF = (0, 0, 3, 1, 3, 1, 2, 2)
Z_OFF = (0, 1, 0, 0, 1, 1, 0, 1)
T = 256
E = 768
H = 384
SPLIT = (7,)


def nt(a, b):
    return lax.dot_general(a, b, (((1,), (1,)), ((), ())), preferred_element_type=F32)


def nn(a, b):
    return lax.dot_general(a, b, (((1,), (0,)), ((), ())), preferred_element_type=F32)


def kernel(
    factor,
    tok_hbm, att_hbm, w_hbm, cot_hbm,
    mixed, gatt, wg,
    tok, a_own, perm, at, w, cot, part,
    bx, br, bfin, bz, gacc,
    term, xr, xfin, xs, zr, zfin, res, resx,
    lsem, ssem, rsem,
):
    dp, tp = lax.axis_index("dp"), lax.axis_index("tensor")
    x, zh, c = dp // 8, (dp // 2) % 4, dp % 2
    y, zl = tp // 2, tp % 2

    def dev(x_, zh_, c_, y_, zl_):
        return ((x_ * 4 + zh_) * 2 + c_, y_ * 2 + zl_)

    xp, xm = dev((x + 1) % 4, zh, c, y, zl), dev((x + 3) % 4, zh, c, y, zl)
    yp, ym = dev(x, zh, c, (y + 1) % 4, zl), dev(x, zh, c, (y + 3) % 4, zl)
    zp, zm = dev(x, (zh + 1) % 4, c, y, zl), dev(x, (zh + 3) % 4, c, y, zl)
    zo, co = dev(x, zh, c, y, 1 - zl), dev(x, zh, 1 - c, y, zl)

    barrier = pltpu.get_barrier_semaphore()
    for to in (xp, xm, yp, ym, zp, zm, zo, co):
        pl.semaphore_signal(barrier, inc=1, device_id=to, device_id_type=MESH)

    def slot(i, k):
        return (0, 2 + k, 3 - k, 1, 6, 4 + k, 5 - k, 7)[i]

    def block(s):
        return ((y + Y_OFF[s]) % 4) * 2 + (zl + Z_OFF[s]) % 2

    def step_block(i, k):
        yo = (0, 3 - 2 * k, 1 + 2 * k, 0, 2, 3 - 2 * k, 1 + 2 * k, 2)[i]
        return ((y + yo) % 4) * 2 + (zl + (0, 0, 0, 1, 0, 1, 1, 1)[i]) % 2

    count = [0]

    def load(src, dst):
        copy = pltpu.make_async_copy(src, dst, lsem.at[count[0]])
        count[0] += 1
        copy.start()
        return copy

    l_cot = [load(cot_hbm.at[:, pl.ds(H * h, H)], cot.at[0, 1 + h]) for h in range(2)]
    l_att = [load(att_hbm.at[h], a_own.at[:, pl.ds(128 * h, 128)]) for h in range(6)]
    sent = []

    def send(src, dst, to):
        i = len(sent)
        copy = pltpu.make_async_remote_copy(
            src_ref=src, dst_ref=dst, send_sem=ssem.at[i], recv_sem=rsem.at[i],
            device_id=to, device_id_type=MESH,
        )
        copy.start()
        sent.append(copy)
        return copy

    a, cx = {}, {}

    def a_send(src, s, h, to):
        a[s, h] = send(cot.at[src, 1 + h], cot.at[s, 1 + h], to)

    def core_send(i):
        s = slot(i, 1 - c)
        cx[i] = send(cot.at[s, 2 - c], cot.at[s, 3 * (1 - c)], co)

    def make_perm(i, _):
        row = lax.broadcasted_iota(jnp.int32, (48, 128), 0)
        core = (row >= 24).astype(jnp.int32)
        r = row - 24 * core
        want = (r >> 2) * 128 + 8 * i + 4 * core + (r & 3)
        want = want - lax.broadcasted_iota(jnp.int32, (48, 128), 1)
        rows = pl.ds(pl.multiple_of((i % 8) * 48, 16), 48)
        for h in range(6):
            perm[i // 8, rows, pl.ds(128 * h, 128)] = (
                jnp.where(want == 128 * h, 1.0, 0.0).astype(BF16)
            )
        return 0

    lax.fori_loop(0, 16, make_perm, 0)
    gacc[...] = jnp.zeros_like(gacc)
    pl.semaphore_wait(barrier, 8)
    l_cot[0].wait()
    l_cot[1].wait()
    a_send(0, 2, 0, yp)
    a_send(0, 3, 1, ym)
    a[1] = send(cot.at[0, pl.ds(1, 2)], cot.at[1, pl.ds(1, 2)], zo)
    core_send(0)
    a_send(0, 2, 1, yp)
    a_send(0, 3, 0, ym)
    l_w = {}
    for s in (7, 5, 4, 2, 3, 6, 1, 0):
        for h in range(2):
            col = pl.multiple_of(block(s) * E + H * h, 128)
            l_w[s, h] = load(w_hbm.at[:, pl.ds(col, H)], w.at[s, h])
    l_tok = load(tok_hbm, tok)

    for cp in l_att:
        cp.wait()
    mine = pl.ds(pl.multiple_of(T * (1 - c), T), T)

    def permute(i, _):
        at[i, :, mine] = nt(perm[i], a_own[...]).astype(BF16)
        return 0

    lax.fori_loop(0, 2, permute, 0)
    a_swap = send(at.at[:, :, mine], at.at[:, :, mine], co)

    x1, x2, zf, zn, zt, r1 = {}, {}, {}, {}, {}, {}
    xf, xn, xl = (x + 2) % 4, (x + 1) % 4, (x + 3) % 4

    def c_term(i):
        cx[i].wait_recv()
        s = slot(i, c)

        val = nn(at[...].reshape(E, 2 * T), cot[s, pl.ds(2 * c, 2)].reshape(2 * T, H))
        term[i] = val.astype(BF16).reshape(4, 4, 48, H)
        for u in range(2 if i in SPLIT else 1):
            p, q = x_parts(i, u)
            x1[i, u] = [
                send(term.at[i, xf, p], xr.at[i, 0, p], xp),
                send(term.at[i, xf, q], xr.at[i, 1, q], xm),
                send(term.at[i, xn, q], xfin.at[i, 0, q], xp),
                send(term.at[i, xl, p], xfin.at[i, 1, p], xm),
            ]

    def x_parts(i, u):
        if i not in SPLIT:
            return pl.ds(0, 2), pl.ds(2, 2)
        n_p, n_m, _, _ = z_places(i)
        p, q = (((zh + 2) % 4, n_p), (n_m, zh))[u]
        return pl.ds(p, 1), pl.ds(q, 1)

    def c_relay(i, u=0):
        p, q = x_parts(i, u)
        x1[i, u][0].wait_recv()
        t = term[i, xn, p].astype(F32) + xr[i, 0, p].astype(F32)
        term[i, xn, p] = t.astype(BF16)
        x2[i, u] = [send(term.at[i, xn, p], xfin.at[i, 0, p], xp)]
        x1[i, u][1].wait_recv()
        t = term[i, xl, q].astype(F32) + xr[i, 1, q].astype(F32)
        term[i, xl, q] = t.astype(BF16)
        x2[i, u].append(send(term.at[i, xl, q], xfin.at[i, 1, q], xm))

    def z_places(i):
        up, down = (zh + 1) % 4, (zh + 3) % 4
        return (up, down, zp, zm) if i % 2 == 0 else (down, up, zm, zp)

    def c_xsum(i, u=0):
        for cp in x1[i, u][2:] + x2[i, u]:
            cp.wait_recv()
        _, n_m, to_p, to_m = z_places(i)
        for part_z in x_parts(i, u) if i in SPLIT else (pl.ds(0, 4),):
            t = term[i, x, part_z].astype(F32) + xfin[i, 0, part_z].astype(F32)
            xs[i, part_z] = (t + xfin[i, 1, part_z].astype(F32)).astype(BF16)
        if u == 0:
            zf[i] = send(xs.at[i, (zh + 2) % 4], zr.at[i], to_p)
        if u == 1 or i not in SPLIT:
            zn[i] = send(xs.at[i, n_m], zfin.at[i, 1], to_m)

    def c_zrelay(i):
        n_p, _, to_p, _ = z_places(i)
        zf[i].wait_recv()
        t = xs[i, n_p].astype(F32) + zr[i].astype(F32)
        xs[i, n_p] = t.astype(BF16)
        zt[i] = send(xs.at[i, n_p], zfin.at[i, 0], to_p)

    def put(val, col):
        cols = pl.ds(pl.multiple_of(col, 128), H)
        for h in range(6):
            wg[h, :, cols] = val[4 * h : 4 * h + 4]

    def c_zsum(i):
        zn[i].wait_recv()
        zt[i].wait_recv()
        t = xs[i, zh].astype(F32) + zfin[i, 0].astype(F32) + zfin[i, 1].astype(F32)
        res[i] = (t * factor).reshape(2, 24, H)
        r1[i] = send(res.at[i, 1 - c], resx.at[i], co)
        put(res[i, c], step_block(i, c) * E + H * c)

    def c_out(i):
        r1[i].wait_recv()
        put(resx[i], step_block(i, 1 - c) * E + H * (1 - c))

    def grad(s):
        def go(b, _):
            cols = pl.ds(pl.multiple_of(b * T, T), T)
            t = nt(cot[s, 1], w[s, 0, cols]) + nt(cot[s, 2], w[s, 1, cols])
            gacc[:, cols] += t
            return 0

        lax.fori_loop(0, 3, go, 0)

    def b_part(s):
        for h in range(2):
            l_w[s, h].wait()

        def go(h, _):
            part[s, h] = nn(a_own[...], w[s, h]).astype(BF16)
            return 0

        lax.fori_loop(0, 2, go, 0)

    b1 = {}

    def b_over():
        b1["x"] = send(part.at[7], bx, zo)

    def b_near(r):
        if r == 0:
            b1["n0"] = [
                send(part.at[5], bfin.at[0, 0], yp),
                send(part.at[4], bfin.at[0, 1], ym),
            ]
        else:
            b1["n1"] = [
                send(part.at[3, 1], bfin.at[1, 0, 1], yp),
                send(part.at[2, 0], bfin.at[1, 1, 0], ym),
            ]

    def add_to(s, h, ref):
        part[s, h] = (part[s, h].astype(F32) + ref[h].astype(F32)).astype(BF16)

    def b_far():
        b1["f"] = []
        b1["x"].wait_recv()
        for h, to in ((0, yp), (1, ym)):
            add_to(6, h, bx)
            b1["f"].append(send(part.at[6, h], br.at[h], to))

    def b_relay():
        b1["r"] = []
        for h, s, to in ((0, 3, yp), (1, 2, ym)):
            b1["f"][h].wait_recv()
            add_to(s, h, br)
            b1["r"].append(send(part.at[s, h], bfin.at[1, h, h], to))

    def b_sum(r, h):
        t = part[1 - r, h].astype(F32) + bfin[r, 0, h].astype(F32)
        return t + bfin[r, 1, h].astype(F32)

    def b_cross():
        for cp in b1["n0"]:
            cp.wait_recv()
        for h in range(2):
            part[1, h] = b_sum(0, h).astype(BF16)
        b1["c"] = send(part.at[1], bz, zo)

    def b_mix():
        for cp in b1["n1"] + b1["r"]:
            cp.wait_recv()
        l_tok.wait()
        b1["c"].wait_recv()
        for h in range(2):
            t = b_sum(1, h) + bz[h].astype(F32)
            cols = pl.ds(H * h, H)
            mixed[:, cols] = (tok[:, cols].astype(F32) + t).astype(BF16)

    def grad_out():
        for h in range(6):
            gatt[h] = gacc[:, pl.ds(128 * h, 128)].astype(BF16)

    drained = [0]

    def drain(n):
        for cp in sent[drained[0] : n]:
            cp.wait_send()
        drained[0] = max(drained[0], n)

    def arrived(*keys):
        for k in keys:
            a[k].wait_recv()

    b_part(7)
    a_swap.wait_recv()
    c_term(0)
    b_part(3)
    b_part(5)
    b_part(4)
    arrived((2, 0), (3, 1))
    a_send(2, 6, 0, yp)
    a_send(3, 6, 1, ym)
    core_send(1)
    c_relay(0)
    b_part(6)
    c_term(1)
    arrived((2, 1), (3, 0))
    core_send(2)
    b_over()
    arrived(1)
    a_send(1, 4, 1, yp)
    a_send(1, 5, 0, ym)
    c_term(2)
    c_relay(1)
    c_xsum(0)
    core_send(3)
    a_send(1, 4, 0, yp)
    a_send(1, 5, 1, ym)
    b_part(2)
    arrived((6, 0), (6, 1))
    core_send(4)
    c_term(3)
    c_relay(2)
    b_near(0)
    b_part(1)
    drain(11)
    arrived((4, 1), (5, 0))
    core_send(6)
    c_xsum(1)
    c_relay(3)
    c_term(6)
    arrived((4, 0), (5, 1))
    a_send(4, 7, 0, yp)
    a_send(5, 7, 1, ym)
    core_send(5)
    grad(1)
    drain(23)
    c_zrelay(0)
    c_xsum(2)
    b_near(1)
    c_term(4)
    c_xsum(3)
    drain(34)
    c_term(5)
    c_relay(6)
    grad(2)
    drain(40)
    c_zrelay(1)
    b_far()
    c_zrelay(2)
    c_zrelay(3)
    c_relay(4)
    b_cross()
    grad(6)
    drain(48)
    arrived((7, 0), (7, 1))
    core_send(7)
    c_relay(5)
    c_term(7)
    grad(4)
    drain(59)
    grad(3)
    c_zsum(3)
    c_xsum(4)
    c_relay(7, 0)
    c_xsum(5)
    drain(66)
    b_part(0)
    c_relay(7, 1)
    grad(7)
    c_xsum(7, 0)
    c_xsum(6)
    b_relay()
    grad(5)
    drain(73)
    c_zrelay(4)
    c_zsum(2)
    c_zrelay(5)
    c_xsum(7, 1)
    c_zsum(0)
    c_zrelay(7)
    c_zrelay(6)
    c_zsum(1)
    drain(81)
    grad(0)
    c_out(1)
    c_out(0)
    grad_out()
    b_mix()
    c_zsum(5)
    c_out(2)
    c_zsum(7)
    c_zsum(4)
    c_zsum(6)
    c_out(7)
    c_out(5)
    c_out(3)
    c_out(4)
    c_out(6)
    drain(len(sent))


N_SEND = 130


def body(tokens, attended, out_weight, cotangent):
    factor = 1.0 / math.sqrt(attended.shape[0] * lax.axis_size("dp"))
    any_spec = pl.BlockSpec(memory_space=pl.ANY)
    vm = pltpu.VMEM
    mixed, gatt, wg = pl.pallas_call(
        functools.partial(kernel, factor),
        out_shape=(
            vm((T, E), BF16),
            vm((6, T, 128), BF16),
            vm((6, 4, 8 * E), F32),
        ),
        in_specs=[any_spec] * 4,
        out_specs=(pl.BlockSpec(memory_space=vm),) * 3,
        scratch_shapes=[
            vm((T, E), BF16),
            vm((T, E), BF16),
            vm((2, H, E), BF16),
            vm((2, H, 2 * T), BF16),
            vm((8, 2, E, H), BF16),
            vm((8, 4, T, H), BF16),
            vm((8, 2, T, H), BF16),
            vm((2, T, H), BF16),
            vm((2, T, H), BF16),
            vm((2, 2, 2, T, H), BF16),
            vm((2, T, H), BF16),
            vm((T, E), F32),
            vm((8, 4, 4, 48, H), BF16),
            vm((8, 2, 4, 48, H), BF16),
            vm((8, 2, 4, 48, H), BF16),
            vm((8, 4, 48, H), BF16),
            vm((8, 48, H), BF16),
            vm((8, 2, 48, H), BF16),
            vm((8, 2, 24, H), F32),
            vm((8, 24, H), F32),
            pltpu.SemaphoreType.DMA((25,)),
            pltpu.SemaphoreType.DMA((N_SEND,)),
            pltpu.SemaphoreType.DMA((N_SEND,)),
        ],
        compiler_params=pltpu.CompilerParams(
            collective_id=0, has_side_effects=True, vmem_limit_bytes=56 * 2**20
        ),
    )(
        tokens,
        jnp.transpose(attended, (1, 0, 2)),
        jnp.transpose(out_weight, (1, 0, 2)).reshape(E, 8 * E),
        cotangent,
    )
    return (
        mixed,
        jnp.transpose(gatt, (1, 0, 2)),
        jnp.transpose(wg, (1, 0, 2)),
    )


def solution(mesh):
    placed = (
        P("dp", "tensor"),
        P("dp", "tensor", None),
        P(None, "tensor", None),
        P("dp", "tensor"),
    )
    return jax.shard_map(
        body,
        mesh=mesh,
        in_specs=placed,
        out_specs=(P("dp", "tensor"), P("dp", "tensor", None), P("dp", "tensor", None)),
        check_vma=False,
    )
```

```python
import functools
import math

import jax
import jax.numpy as jnp
from jax import lax
from jax.experimental import pallas as pl
from jax.experimental.pallas import tpu as pltpu
from jax.sharding import PartitionSpec as P

MESH = pl.DeviceIdType.MESH
F32 = jnp.float32
BF16 = jnp.bfloat16

Y_OFF = (0, 0, 3, 1, 3, 1, 2, 2)
Z_OFF = (0, 1, 0, 0, 1, 1, 0, 1)
T = 256
E = 768
H = 384
SPLIT = (7,)


def nt(a, b):
    return lax.dot_general(a, b, (((1,), (1,)), ((), ())), preferred_element_type=F32)


def nn(a, b):
    return lax.dot_general(a, b, (((1,), (0,)), ((), ())), preferred_element_type=F32)


def kernel(
    factor,
    tok_hbm, att_hbm, w_hbm, cot_hbm,
    mixed, gatt, wg,
    tok, a_own, perm, at, w, cot, part,
    bx, br, bfin, bz, gacc,
    term, xr, xfin, xs, zr, zfin, res, resx,
    lsem, ssem, rsem,
):
    dp, tp = lax.axis_index("dp"), lax.axis_index("tensor")
    x, zh, c = dp // 8, (dp // 2) % 4, dp % 2
    y, zl = tp // 2, tp % 2

    def dev(x_, zh_, c_, y_, zl_):
        return ((x_ * 4 + zh_) * 2 + c_, y_ * 2 + zl_)

    xp, xm = dev((x + 1) % 4, zh, c, y, zl), dev((x + 3) % 4, zh, c, y, zl)
    yp, ym = dev(x, zh, c, (y + 1) % 4, zl), dev(x, zh, c, (y + 3) % 4, zl)
    zp, zm = dev(x, (zh + 1) % 4, c, y, zl), dev(x, (zh + 3) % 4, c, y, zl)
    zo, co = dev(x, zh, c, y, 1 - zl), dev(x, zh, 1 - c, y, zl)

    barrier = pltpu.get_barrier_semaphore()
    for to in (xp, xm, yp, ym, zp, zm, zo, co):
        pl.semaphore_signal(barrier, inc=1, device_id=to, device_id_type=MESH)

    def slot(i, k):
        return (0, 2 + k, 3 - k, 1, 6, 4 + k, 5 - k, 7)[i]

    def block(s):
        return ((y + Y_OFF[s]) % 4) * 2 + (zl + Z_OFF[s]) % 2

    def step_block(i, k):
        yo = (0, 3 - 2 * k, 1 + 2 * k, 0, 2, 3 - 2 * k, 1 + 2 * k, 2)[i]
        return ((y + yo) % 4) * 2 + (zl + (0, 0, 0, 1, 0, 1, 1, 1)[i]) % 2

    count = [0]

    def load(src, dst):
        copy = pltpu.make_async_copy(src, dst, lsem.at[count[0]])
        count[0] += 1
        copy.start()
        return copy

    l_cot = [load(cot_hbm.at[:, pl.ds(H * h, H)], cot.at[0, 1 + h]) for h in range(2)]
    l_att = [load(att_hbm.at[h], a_own.at[:, pl.ds(128 * h, 128)]) for h in range(6)]
    sent = []

    def send(src, dst, to):
        i = len(sent)
        copy = pltpu.make_async_remote_copy(
            src_ref=src, dst_ref=dst, send_sem=ssem.at[i], recv_sem=rsem.at[i],
            device_id=to, device_id_type=MESH,
        )
        copy.start()
        sent.append(copy)
        return copy

    a, cx = {}, {}

    def a_send(src, s, h, to):
        a[s, h] = send(cot.at[src, 1 + h], cot.at[s, 1 + h], to)

    def core_send(i):
        s = slot(i, 1 - c)
        cx[i] = send(cot.at[s, 2 - c], cot.at[s, 3 * (1 - c)], co)

    def make_perm(i, _):
        row = lax.broadcasted_iota(jnp.int32, (48, 128), 0)
        core = (row >= 24).astype(jnp.int32)
        r = row - 24 * core
        want = (r >> 2) * 128 + 8 * i + 4 * core + (r & 3)
        want = want - lax.broadcasted_iota(jnp.int32, (48, 128), 1)
        rows = pl.ds(pl.multiple_of((i % 8) * 48, 16), 48)
        for h in range(6):
            perm[i // 8, rows, pl.ds(128 * h, 128)] = (
                jnp.where(want == 128 * h, 1.0, 0.0).astype(BF16)
            )
        return 0

    lax.fori_loop(0, 16, make_perm, 0)
    gacc[...] = jnp.zeros_like(gacc)
    pl.semaphore_wait(barrier, 8)
    l_cot[0].wait()
    l_cot[1].wait()
    a_send(0, 2, 0, yp)
    a_send(0, 3, 1, ym)
    a[1] = send(cot.at[0, pl.ds(1, 2)], cot.at[1, pl.ds(1, 2)], zo)
    core_send(0)
    a_send(0, 2, 1, yp)
    a_send(0, 3, 0, ym)
    l_w = {}
    for s in (7, 5, 4, 2, 3, 6, 1, 0):
        for h in range(2):
            col = pl.multiple_of(block(s) * E + H * h, 128)
            l_w[s, h] = load(w_hbm.at[:, pl.ds(col, H)], w.at[s, h])
    l_tok = load(tok_hbm, tok)

    for cp in l_att:
        cp.wait()
    mine = pl.ds(pl.multiple_of(T * (1 - c), T), T)

    def permute(i, _):
        at[i, :, mine] = nt(perm[i], a_own[...]).astype(BF16)
        return 0

    lax.fori_loop(0, 2, permute, 0)
    a_swap = send(at.at[:, :, mine], at.at[:, :, mine], co)

    x1, x2, zf, zn, zt, r1 = {}, {}, {}, {}, {}, {}
    xf, xn, xl = (x + 2) % 4, (x + 1) % 4, (x + 3) % 4

    def c_term(i):
        cx[i].wait_recv()
        s = slot(i, c)

        val = nn(at[...].reshape(E, 2 * T), cot[s, pl.ds(2 * c, 2)].reshape(2 * T, H))
        term[i] = val.astype(BF16).reshape(4, 4, 48, H)
        parts = [x_parts(i, u) for u in range(2 if i in SPLIT else 1)]
        for u, (p, q) in enumerate(parts):
            x1[i, u] = [
                send(term.at[i, xf, p], xr.at[i, 0, p], xp),
                send(term.at[i, xf, q], xr.at[i, 1, q], xm),
            ]
        for u, (p, q) in enumerate(parts):
            x1[i, u] += [
                send(term.at[i, xn, q], xfin.at[i, 0, q], xp),
                send(term.at[i, xl, p], xfin.at[i, 1, p], xm),
            ]

    def x_parts(i, u):
        if i not in SPLIT:
            return pl.ds(0, 2), pl.ds(2, 2)
        n_p, n_m, _, _ = z_places(i)
        p, q = (((zh + 2) % 4, n_p), (n_m, zh))[u]
        return pl.ds(p, 1), pl.ds(q, 1)

    def c_relay(i, u=0):
        p, q = x_parts(i, u)
        x1[i, u][0].wait_recv()
        t = term[i, xn, p].astype(F32) + xr[i, 0, p].astype(F32)
        term[i, xn, p] = t.astype(BF16)
        x2[i, u] = [send(term.at[i, xn, p], xfin.at[i, 0, p], xp)]
        x1[i, u][1].wait_recv()
        t = term[i, xl, q].astype(F32) + xr[i, 1, q].astype(F32)
        term[i, xl, q] = t.astype(BF16)
        x2[i, u].append(send(term.at[i, xl, q], xfin.at[i, 1, q], xm))

    def z_places(i):
        up, down = (zh + 1) % 4, (zh + 3) % 4
        return (up, down, zp, zm) if i % 2 == 0 else (down, up, zm, zp)

    def c_xsum(i, u=0):
        for cp in x1[i, u][2:] + x2[i, u]:
            cp.wait_recv()
        _, n_m, to_p, to_m = z_places(i)
        for part_z in x_parts(i, u) if i in SPLIT else (pl.ds(0, 4),):
            t = term[i, x, part_z].astype(F32) + xfin[i, 0, part_z].astype(F32)
            xs[i, part_z] = (t + xfin[i, 1, part_z].astype(F32)).astype(BF16)
        if u == 0:
            zf[i] = send(xs.at[i, (zh + 2) % 4], zr.at[i], to_p)
        if u == 1 or i not in SPLIT:
            zn[i] = send(xs.at[i, n_m], zfin.at[i, 1], to_m)

    def c_zrelay(i):
        n_p, _, to_p, _ = z_places(i)
        zf[i].wait_recv()
        t = xs[i, n_p].astype(F32) + zr[i].astype(F32)
        xs[i, n_p] = t.astype(BF16)
        zt[i] = send(xs.at[i, n_p], zfin.at[i, 0], to_p)

    def put(val, col):
        cols = pl.ds(pl.multiple_of(col, 128), H)
        for h in range(6):
            wg[h, :, cols] = val[4 * h : 4 * h + 4]

    def c_zsum(i):
        zn[i].wait_recv()
        zt[i].wait_recv()
        t = xs[i, zh].astype(F32) + zfin[i, 0].astype(F32) + zfin[i, 1].astype(F32)
        res[i] = (t * factor).reshape(2, 24, H)
        r1[i] = send(res.at[i, 1 - c], resx.at[i], co)
        put(res[i, c], step_block(i, c) * E + H * c)

    def c_out(i):
        r1[i].wait_recv()
        put(resx[i], step_block(i, 1 - c) * E + H * (1 - c))

    def grad(s):
        def go(b, _):
            cols = pl.ds(pl.multiple_of(b * T, T), T)
            t = nt(cot[s, 1], w[s, 0, cols]) + nt(cot[s, 2], w[s, 1, cols])
            gacc[:, cols] += t
            return 0

        lax.fori_loop(0, 3, go, 0)

    def b_part(s):
        for h in range(2):
            l_w[s, h].wait()

        def go(h, _):
            part[s, h] = nn(a_own[...], w[s, h]).astype(BF16)
            return 0

        lax.fori_loop(0, 2, go, 0)

    b1 = {}

    def b_over(h):
        b1["x", h] = send(part.at[7, h], bx.at[h], zo)

    def b_near(h):
        b1["n", h] = [
            send(part.at[5, h], bfin.at[0, 0, h], yp),
            send(part.at[4, h], bfin.at[0, 1, h], ym),
        ]

    def b_beside():
        b1["b"] = [
            send(part.at[3, 1], bfin.at[1, 0, 1], yp),
            send(part.at[2, 0], bfin.at[1, 1, 0], ym),
        ]

    def add_to(s, h, ref):
        part[s, h] = (part[s, h].astype(F32) + ref[h].astype(F32)).astype(BF16)

    def b_far():
        b1["f"] = []
        for h, to in ((0, yp), (1, ym)):
            b1["x", h].wait_recv()
            add_to(6, h, bx)
            b1["f"].append(send(part.at[6, h], br.at[h], to))

    def b_relay():
        b1["r"] = []
        for h, s, to in ((0, 3, yp), (1, 2, ym)):
            b1["f"][h].wait_recv()
            add_to(s, h, br)
            b1["r"].append(send(part.at[s, h], bfin.at[1, h, h], to))

    def b_sum(r, h, rows=slice(None)):
        t = part[1 - r, h, rows].astype(F32) + bfin[r, 0, h, rows].astype(F32)
        return t + bfin[r, 1, h, rows].astype(F32)

    def b_cross(h, k):
        for cp in b1.pop(("n", h), ()):
            cp.wait_recv()
        rows = pl.ds(k * (T // 2), T // 2)
        part[1, h, rows] = b_sum(0, h, rows).astype(BF16)
        b1["c", h, k] = send(part.at[1, h, rows], bz.at[h, rows], zo)

    def b_mix():
        for cp in b1["b"] + b1["r"]:
            cp.wait_recv()
        l_tok.wait()
        for h in range(2):
            b1["c", h, 0].wait_recv()
            b1["c", h, 1].wait_recv()
            t = b_sum(1, h) + bz[h].astype(F32)
            cols = pl.ds(H * h, H)
            mixed[:, cols] = (tok[:, cols].astype(F32) + t).astype(BF16)

    def grad_out():
        for h in range(6):
            gatt[h] = gacc[:, pl.ds(128 * h, 128)].astype(BF16)

    drained = [0]

    def drain(n):
        for cp in sent[drained[0] : n]:
            cp.wait_send()
        drained[0] = max(drained[0], n)

    def arrived(*keys):
        for k in keys:
            a[k].wait_recv()

    b_part(7)
    b_part(3)
    a_swap.wait_recv()
    c_term(0)
    b_part(4)
    b_part(5)
    b_over(1)
    b_near(0)
    arrived((2, 0), (3, 1))
    a_send(2, 6, 0, yp)
    a_send(3, 6, 1, ym)
    core_send(1)
    b_part(2)
    c_relay(0)
    c_term(1)
    b_part(1)
    arrived(1)
    core_send(3)
    arrived((2, 1), (3, 0))
    core_send(2)
    grad(1)
    c_term(3)
    c_xsum(0)
    a_send(1, 4, 0, yp)
    a_send(1, 5, 1, ym)
    c_term(2)
    grad(2)
    b_cross(0, 1)
    a_send(1, 4, 1, yp)
    a_send(1, 5, 0, ym)
    b_part(6)
    drain(7)
    b_cross(0, 0)
    c_zrelay(0)
    c_relay(3)
    b_over(0)
    b_near(1)
    c_relay(1)
    arrived((6, 0), (6, 1))
    core_send(4)
    grad(3)
    drain(17)
    c_relay(2)
    c_term(4)
    arrived((4, 0), (5, 1))
    a_send(4, 7, 0, yp)
    a_send(5, 7, 1, ym)
    core_send(5)
    c_xsum(3)
    drain(28)
    c_xsum(1)
    c_term(5)
    c_xsum(2)
    drain(36)
    b_part(0)
    arrived((4, 1), (5, 0))
    core_send(6)
    grad(0)
    c_relay(4)
    c_term(6)
    c_zrelay(3)
    b_cross(1, 1)
    c_zsum(0)
    drain(46)
    b_far()
    c_relay(5)
    grad(6)
    b_beside()
    c_xsum(4)
    drain(54)
    arrived((7, 0), (7, 1))
    core_send(7)
    b_cross(1, 0)
    c_relay(6)
    c_zrelay(2)
    c_term(7)
    c_zrelay(1)
    c_xsum(5)
    drain(70)
    grad(4)
    c_relay(7, 0)
    c_xsum(6)
    c_relay(7, 1)
    b_relay()
    c_out(0)
    drain(78)
    grad(5)
    c_zrelay(4)
    c_xsum(7, 0)
    c_zsum(2)
    c_zrelay(6)
    c_zrelay(5)
    c_zsum(3)
    drain(84)
    grad(7)
    c_xsum(7, 1)
    c_zrelay(7)
    c_zsum(6)
    c_out(3)
    c_zsum(4)
    c_zsum(1)
    grad_out()
    c_zsum(5)
    drain(90)
    b_mix()
    c_zsum(7)
    c_out(1)
    c_out(6)
    c_out(2)
    c_out(5)
    c_out(4)
    c_out(7)
    drain(len(sent))


N_SEND = 130


def body(tokens, attended, out_weight, cotangent):
    factor = 1.0 / math.sqrt(attended.shape[0] * lax.axis_size("dp"))
    any_spec = pl.BlockSpec(memory_space=pl.ANY)
    vm = pltpu.VMEM
    mixed, gatt, wg = pl.pallas_call(
        functools.partial(kernel, factor),
        out_shape=(
            vm((T, E), BF16),
            vm((6, T, 128), BF16),
            vm((6, 4, 8 * E), F32),
        ),
        in_specs=[any_spec] * 4,
        out_specs=(pl.BlockSpec(memory_space=vm),) * 3,
        scratch_shapes=[
            vm((T, E), BF16),
            vm((T, E), BF16),
            vm((2, H, E), BF16),
            vm((2, H, 2 * T), BF16),
            vm((8, 2, E, H), BF16),
            vm((8, 4, T, H), BF16),
            vm((8, 2, T, H), BF16),
            vm((2, T, H), BF16),
            vm((2, T, H), BF16),
            vm((2, 2, 2, T, H), BF16),
            vm((2, T, H), BF16),
            vm((T, E), F32),
            vm((8, 4, 4, 48, H), BF16),
            vm((8, 2, 4, 48, H), BF16),
            vm((8, 2, 4, 48, H), BF16),
            vm((8, 4, 48, H), BF16),
            vm((8, 48, H), BF16),
            vm((8, 2, 48, H), BF16),
            vm((8, 2, 24, H), F32),
            vm((8, 24, H), F32),
            pltpu.SemaphoreType.DMA((25,)),
            pltpu.SemaphoreType.DMA((N_SEND,)),
            pltpu.SemaphoreType.DMA((N_SEND,)),
        ],
        compiler_params=pltpu.CompilerParams(
            collective_id=0, has_side_effects=True, vmem_limit_bytes=56 * 2**20
        ),
    )(
        tokens,
        jnp.transpose(attended, (1, 0, 2)),
        jnp.transpose(out_weight, (1, 0, 2)).reshape(E, 8 * E),
        cotangent,
    )
    return (
        mixed,
        jnp.transpose(gatt, (1, 0, 2)),
        jnp.transpose(wg, (1, 0, 2)),
    )


def solution(mesh):
    placed = (
        P("dp", "tensor"),
        P("dp", "tensor", None),
        P(None, "tensor", None),
        P("dp", "tensor"),
    )
    return jax.shard_map(
        body,
        mesh=mesh,
        in_specs=placed,
        out_specs=(P("dp", "tensor"), P("dp", "tensor", None), P("dp", "tensor", None)),
        check_vma=False,
    )
```

```python
import functools
import math

import jax
import jax.numpy as jnp
from jax import lax
from jax.experimental import pallas as pl
from jax.experimental.pallas import tpu as pltpu
from jax.sharding import PartitionSpec as P

MESH = pl.DeviceIdType.MESH
F32 = jnp.float32
BF16 = jnp.bfloat16

Y_OFF = (0, 0, 3, 1, 3, 1, 2, 2)
Z_OFF = (0, 1, 0, 0, 1, 1, 0, 1)
T = 256
E = 768
H = 384
SPLIT = (6, 7, )


def nt(a, b):
    return lax.dot_general(a, b, (((1,), (1,)), ((), ())), preferred_element_type=F32)


def nn(a, b):
    return lax.dot_general(a, b, (((1,), (0,)), ((), ())), preferred_element_type=F32)


def kernel(
    factor,
    tok_hbm, att_hbm, w_hbm, cot_hbm,
    mixed, gatt, wg,
    tok, a_own, perm, at, w, cot, part,
    bx, br, bfin, bz, gacc,
    term, xr, xfin, xs, zr, zfin, res, resx,
    lsem, ssem, rsem,
):
    dp, tp = lax.axis_index("dp"), lax.axis_index("tensor")
    x, zh, c = dp // 8, (dp // 2) % 4, dp % 2
    y, zl = tp // 2, tp % 2

    def dev(x_, zh_, c_, y_, zl_):
        return ((x_ * 4 + zh_) * 2 + c_, y_ * 2 + zl_)

    xp, xm = dev((x + 1) % 4, zh, c, y, zl), dev((x + 3) % 4, zh, c, y, zl)
    yp, ym = dev(x, zh, c, (y + 1) % 4, zl), dev(x, zh, c, (y + 3) % 4, zl)
    zp, zm = dev(x, (zh + 1) % 4, c, y, zl), dev(x, (zh + 3) % 4, c, y, zl)
    zo, co = dev(x, zh, c, y, 1 - zl), dev(x, zh, 1 - c, y, zl)

    barrier = pltpu.get_barrier_semaphore()
    for to in (xp, xm, yp, ym, zp, zm, zo, co):
        pl.semaphore_signal(barrier, inc=1, device_id=to, device_id_type=MESH)

    def slot(i, k):
        return (0, 2 + k, 3 - k, 1, 6, 4 + k, 5 - k, 7)[i]

    def block(s):
        return ((y + Y_OFF[s]) % 4) * 2 + (zl + Z_OFF[s]) % 2

    def step_block(i, k):
        yo = (0, 3 - 2 * k, 1 + 2 * k, 0, 2, 3 - 2 * k, 1 + 2 * k, 2)[i]
        return ((y + yo) % 4) * 2 + (zl + (0, 0, 0, 1, 0, 1, 1, 1)[i]) % 2

    count = [0]

    def load(src, dst):
        copy = pltpu.make_async_copy(src, dst, lsem.at[count[0]])
        count[0] += 1
        copy.start()
        return copy

    l_cot = [load(cot_hbm.at[:, pl.ds(H * h, H)], cot.at[0, 1 + h]) for h in range(2)]
    l_att = [load(att_hbm.at[h], a_own.at[:, pl.ds(128 * h, 128)]) for h in range(6)]
    sent = []

    def send(src, dst, to):
        i = len(sent)
        copy = pltpu.make_async_remote_copy(
            src_ref=src, dst_ref=dst, send_sem=ssem.at[i], recv_sem=rsem.at[i],
            device_id=to, device_id_type=MESH,
        )
        copy.start()
        sent.append(copy)
        return copy

    a, cx = {}, {}

    def a_send(src, s, h, to):
        a[s, h] = send(cot.at[src, 1 + h], cot.at[s, 1 + h], to)

    def core_send(i):
        s = slot(i, 1 - c)
        cx[i] = send(cot.at[s, 2 - c], cot.at[s, 3 * (1 - c)], co)

    def make_perm(i, _):
        row = lax.broadcasted_iota(jnp.int32, (48, 128), 0)
        core = (row >= 24).astype(jnp.int32)
        r = row - 24 * core
        want = (r >> 2) * 128 + 8 * i + 4 * core + (r & 3)
        want = want - lax.broadcasted_iota(jnp.int32, (48, 128), 1)
        rows = pl.ds(pl.multiple_of((i % 8) * 48, 16), 48)
        for h in range(6):
            perm[i // 8, rows, pl.ds(128 * h, 128)] = (
                jnp.where(want == 128 * h, 1.0, 0.0).astype(BF16)
            )
        return 0

    lax.fori_loop(0, 16, make_perm, 0)
    gacc[...] = jnp.zeros_like(gacc)
    pl.semaphore_wait(barrier, 8)
    l_cot[0].wait()
    l_cot[1].wait()
    a_send(0, 2, 0, yp)
    a_send(0, 3, 1, ym)
    a[1] = [send(cot.at[0, pl.ds(1, 2)], cot.at[1, pl.ds(1, 2)], zo)]
    core_send(0)
    a_send(0, 2, 1, yp)
    a_send(0, 3, 0, ym)
    l_w = {}
    for s in (7, 5, 4, 2, 3, 6, 1, 0):
        for h in range(2):
            col = pl.multiple_of(block(s) * E + H * h, 128)
            l_w[s, h] = load(w_hbm.at[:, pl.ds(col, H)], w.at[s, h])
    l_tok = load(tok_hbm, tok)

    for cp in l_att:
        cp.wait()
    mine = pl.ds(pl.multiple_of(T * (1 - c), T), T)

    a_swap = []
    for i in range(2):
        at[i, :, mine] = nt(perm[i], a_own[...]).astype(BF16)
        a_swap.append(send(at.at[i, :, mine], at.at[i, :, mine], co))

    x1, x2, zf, zn, zt, r1 = {}, {}, {}, {}, {}, {}
    xf, xn, xl = (x + 2) % 4, (x + 1) % 4, (x + 3) % 4

    def c_term(i):
        cx[i].wait_recv()
        s = slot(i, c)

        val = nn(at[...].reshape(E, 2 * T), cot[s, pl.ds(2 * c, 2)].reshape(2 * T, H))
        term[i] = val.astype(BF16).reshape(4, 4, 48, H)
        parts = [x_parts(i, u) for u in range(2 if i in SPLIT else 1)]
        for u, (p, q) in enumerate(parts):
            x1[i, u] = [
                send(term.at[i, xf, p], xr.at[i, 0, p], xp),
                send(term.at[i, xf, q], xr.at[i, 1, q], xm),
            ]

    def c_near(i, u=0):
        p, q = x_parts(i, u)
        x1[i, u] += [
            send(term.at[i, xn, q], xfin.at[i, 0, q], xp),
            send(term.at[i, xl, p], xfin.at[i, 1, p], xm),
        ]

    def x_parts(i, u):
        if i not in SPLIT:
            return pl.ds(0, 2), pl.ds(2, 2)
        n_p, n_m, _, _ = z_places(i)
        p, q = (((zh + 2) % 4, n_p), (n_m, zh))[u]
        return pl.ds(p, 1), pl.ds(q, 1)

    def c_relay(i, u=0):
        p, q = x_parts(i, u)
        x1[i, u][0].wait_recv()
        t = term[i, xn, p].astype(F32) + xr[i, 0, p].astype(F32)
        term[i, xn, p] = t.astype(BF16)
        x2[i, u] = [send(term.at[i, xn, p], xfin.at[i, 0, p], xp)]
        x1[i, u][1].wait_recv()
        t = term[i, xl, q].astype(F32) + xr[i, 1, q].astype(F32)
        term[i, xl, q] = t.astype(BF16)
        x2[i, u].append(send(term.at[i, xl, q], xfin.at[i, 1, q], xm))

    def z_places(i):
        way = 1 + 2 * ((i + zl + 1) % 2)
        n_p, n_m = (zh + way) % 4, (zh + 4 - way) % 4
        return n_p, n_m, dev(x, n_p, c, y, zl), dev(x, n_m, c, y, zl)

    def c_xsum(i, u=0):
        for cp in x1[i, u][2:] + x2[i, u]:
            cp.wait_recv()
        _, n_m, to_p, to_m = z_places(i)
        for part_z in x_parts(i, u) if i in SPLIT else (pl.ds(0, 4),):
            t = term[i, x, part_z].astype(F32) + xfin[i, 0, part_z].astype(F32)
            xs[i, part_z] = (t + xfin[i, 1, part_z].astype(F32)).astype(BF16)
        if u == 0:
            zf[i] = send(xs.at[i, (zh + 2) % 4], zr.at[i], to_p)
        if u == 1 or i not in SPLIT:
            zn[i] = send(xs.at[i, n_m], zfin.at[i, 1], to_m)

    def c_zrelay(i):
        n_p, _, to_p, _ = z_places(i)
        zf[i].wait_recv()
        t = xs[i, n_p].astype(F32) + zr[i].astype(F32)
        xs[i, n_p] = t.astype(BF16)
        zt[i] = send(xs.at[i, n_p], zfin.at[i, 0], to_p)

    def put(val, col):
        cols = pl.ds(pl.multiple_of(col, 128), H)
        for h in range(6):
            wg[h, :, cols] = val[4 * h : 4 * h + 4]

    def c_zsum(i):
        zn[i].wait_recv()
        zt[i].wait_recv()
        t = xs[i, zh].astype(F32) + zfin[i, 0].astype(F32) + zfin[i, 1].astype(F32)
        res[i] = (t * factor).reshape(2, 24, H)
        r1[i] = send(res.at[i, 1 - c], resx.at[i], co)
        put(res[i, c], step_block(i, c) * E + H * c)

    def c_out(i):
        r1[i].wait_recv()
        put(resx[i], step_block(i, 1 - c) * E + H * (1 - c))

    def w_ready(s):
        for h in range(2):
            if (s, h) in l_w:
                l_w.pop((s, h)).wait()

    def grad(s):
        w_ready(s)

        def go(b, _):
            cols = pl.ds(pl.multiple_of(b * T, T), T)
            t = nt(cot[s, 1], w[s, 0, cols]) + nt(cot[s, 2], w[s, 1, cols])
            gacc[:, cols] += t
            return 0

        lax.fori_loop(0, 3, go, 0)

    def b_part(s):
        w_ready(s)

        def go(h, _):
            part[s, h] = nn(a_own[...], w[s, h]).astype(BF16)
            return 0

        lax.fori_loop(0, 2, go, 0)

    b1 = {}

    def b_over(h):
        b1["x", h] = send(part.at[7, h], bx.at[h], zo)

    def b_near(h):
        b1["n", h] = [
            send(part.at[5, h], bfin.at[0, 0, h], yp),
            send(part.at[4, h], bfin.at[0, 1, h], ym),
        ]

    def b_beside():
        b1["b"] = [
            send(part.at[3, 1], bfin.at[1, 0, 1], yp),
            send(part.at[2, 0], bfin.at[1, 1, 0], ym),
        ]

    def add_to(s, h, ref):
        part[s, h] = (part[s, h].astype(F32) + ref[h].astype(F32)).astype(BF16)

    def b_far():
        b1["f"] = []
        for h, to in ((0, yp), (1, ym)):
            b1["x", h].wait_recv()
            add_to(6, h, bx)
            b1["f"].append(send(part.at[6, h], br.at[h], to))

    def b_relay():
        b1["r"] = []
        for h, s, to in ((0, 3, yp), (1, 2, ym)):
            b1["f"][h].wait_recv()
            add_to(s, h, br)
            b1["r"].append(send(part.at[s, h], bfin.at[1, h, h], to))

    def b_sum(r, h, rows=slice(None)):
        t = part[1 - r, h, rows].astype(F32) + bfin[r, 0, h, rows].astype(F32)
        return t + bfin[r, 1, h, rows].astype(F32)

    def b_cross(h, k):
        for cp in b1.pop(("n", h), ()):
            cp.wait_recv()
        rows = pl.ds(k * (T // 2), T // 2)
        part[1, h, rows] = b_sum(0, h, rows).astype(BF16)
        b1["c", h, k] = send(part.at[1, h, rows], bz.at[h, rows], zo)

    def b_mix():
        for cp in b1["b"] + b1["r"]:
            cp.wait_recv()
        l_tok.wait()
        for h in range(2):
            b1["c", h, 0].wait_recv()
            b1["c", h, 1].wait_recv()
            t = b_sum(1, h) + bz[h].astype(F32)
            cols = pl.ds(H * h, H)
            mixed[:, cols] = (tok[:, cols].astype(F32) + t).astype(BF16)

    def grad_out():
        for h in range(6):
            gatt[h] = gacc[:, pl.ds(128 * h, 128)].astype(BF16)

    drained = [0]

    def drain(n):
        for cp in sent[drained[0] : n]:
            cp.wait_send()
        drained[0] = max(drained[0], n)

    def arrived(*keys):
        for k in keys:
            for cp in a[k] if k == 1 else [a[k]]:
                cp.wait_recv()

    b_part(7)
    for cp in a_swap:
        cp.wait_recv()
    c_term(0)
    c_near(0)
    b_part(4)
    b_part(5)
    grad(0)
    arrived((2, 0), (3, 1))
    a_send(2, 6, 0, yp)
    a_send(3, 6, 1, ym)
    core_send(1)
    c_relay(0)
    c_term(1)
    c_near(1)
    arrived(1)
    core_send(3)
    b_part(1)
    a_send(1, 4, 0, yp)
    a_send(1, 5, 1, ym)
    b_over(0)
    c_term(3)
    c_near(3)
    c_xsum(0)
    c_relay(1)
    b_part(6)
    b_near(0)
    arrived((6, 0), (6, 1))
    core_send(4)
    b_over(1)
    a_send(1, 4, 1, yp)
    a_send(1, 5, 0, ym)
    arrived((2, 1), (3, 0))
    core_send(2)
    grad(3)
    drain(7)
    c_relay(3)
    c_term(4)
    arrived((4, 0), (5, 1))
    a_send(4, 7, 0, yp)
    a_send(5, 7, 1, ym)
    core_send(5)
    b_part(3)
    drain(14)
    c_near(4)
    c_xsum(1)
    c_term(5)
    b_part(2)
    drain(20)
    c_xsum(3)
    b_cross(0, 1)
    c_relay(4)
    c_term(2)
    b_cross(0, 0)
    grad(1)
    drain(28)
    c_near(5)
    b_near(1)
    c_relay(5)
    c_zrelay(1)
    c_near(2)
    arrived((4, 1), (5, 0))
    core_send(6)
    c_xsum(4)
    drain(40)
    b_part(0)
    c_zrelay(0)
    c_term(6)
    c_relay(2)
    c_zrelay(3)
    arrived((7, 0), (7, 1))
    core_send(7)
    c_zrelay(4)
    c_near(6, 0)
    b_far()
    c_xsum(5)
    drain(56)
    c_term(7)
    c_relay(6, 0)
    b_cross(1, 1)
    b_cross(1, 0)
    c_near(7, 0)
    grad(4)
    drain(66)
    c_relay(6, 1)
    c_xsum(2)
    c_zsum(4)
    c_relay(7, 0)
    b_beside()
    c_zrelay(5)
    c_zsum(3)
    drain(77)
    c_near(6, 1)
    c_relay(7, 1)
    c_xsum(6, 0)
    c_near(7, 1)
    grad(6)
    drain(84)
    c_zsum(1)
    c_xsum(7, 0)
    b_relay()
    c_out(3)
    c_xsum(6, 1)
    c_zrelay(2)
    c_zsum(0)
    drain(91)
    grad(2)
    c_zrelay(6)
    c_zsum(5)
    c_xsum(7, 1)
    c_zrelay(7)
    grad(5)
    c_out(0)
    c_out(4)
    c_zsum(2)
    grad(7)
    c_out(2)
    grad_out()
    c_out(1)
    c_zsum(6)
    drain(97)
    c_out(5)
    c_zsum(7)
    b_mix()
    c_out(6)
    c_out(7)
    drain(len(sent))


N_SEND = 144


def body(tokens, attended, out_weight, cotangent):
    factor = 1.0 / math.sqrt(attended.shape[0] * lax.axis_size("dp"))
    any_spec = pl.BlockSpec(memory_space=pl.ANY)
    vm = pltpu.VMEM
    mixed, gatt, wg = pl.pallas_call(
        functools.partial(kernel, factor),
        out_shape=(
            vm((T, E), BF16),
            vm((6, T, 128), BF16),
            vm((6, 4, 8 * E), F32),
        ),
        in_specs=[any_spec] * 4,
        out_specs=(pl.BlockSpec(memory_space=vm),) * 3,
        scratch_shapes=[
            vm((T, E), BF16),
            vm((T, E), BF16),
            vm((2, H, E), BF16),
            vm((2, H, 2 * T), BF16),
            vm((8, 2, E, H), BF16),
            vm((8, 4, T, H), BF16),
            vm((8, 2, T, H), BF16),
            vm((2, T, H), BF16),
            vm((2, T, H), BF16),
            vm((2, 2, 2, T, H), BF16),
            vm((2, T, H), BF16),
            vm((T, E), F32),
            vm((8, 4, 4, 48, H), BF16),
            vm((8, 2, 4, 48, H), BF16),
            vm((8, 2, 4, 48, H), BF16),
            vm((8, 4, 48, H), BF16),
            vm((8, 48, H), BF16),
            vm((8, 2, 48, H), BF16),
            vm((8, 2, 24, H), F32),
            vm((8, 24, H), F32),
            pltpu.SemaphoreType.DMA((25,)),
            pltpu.SemaphoreType.DMA((N_SEND,)),
            pltpu.SemaphoreType.DMA((N_SEND,)),
        ],
        compiler_params=pltpu.CompilerParams(
            collective_id=0, has_side_effects=True, vmem_limit_bytes=56 * 2**20
        ),
    )(
        tokens,
        jnp.transpose(attended, (1, 0, 2)),
        jnp.transpose(out_weight, (1, 0, 2)).reshape(E, 8 * E),
        cotangent,
    )
    return (
        mixed,
        jnp.transpose(gatt, (1, 0, 2)),
        jnp.transpose(wg, (1, 0, 2)),
    )


def solution(mesh):
    placed = (
        P("dp", "tensor"),
        P("dp", "tensor", None),
        P(None, "tensor", None),
        P("dp", "tensor"),
    )
    return jax.shard_map(
        body,
        mesh=mesh,
        in_specs=placed,
        out_specs=(P("dp", "tensor"), P("dp", "tensor", None), P("dp", "tensor", None)),
        check_vma=False,
    )
```

```python
import functools
import math

import jax
import jax.numpy as jnp
from jax import lax
from jax.experimental import pallas as pl
from jax.experimental.pallas import tpu as pltpu
from jax.sharding import PartitionSpec as P

MESH = pl.DeviceIdType.MESH
F32 = jnp.float32
BF16 = jnp.bfloat16

Y_OFF = (0, 0, 3, 1, 3, 1, 2, 2)
Z_OFF = (0, 1, 0, 0, 1, 1, 0, 1)
T = 256
E = 768
H = 384
SPLIT = (6, 7, )


def nt(a, b):
    return lax.dot_general(a, b, (((1,), (1,)), ((), ())), preferred_element_type=F32)


def nn(a, b):
    return lax.dot_general(a, b, (((1,), (0,)), ((), ())), preferred_element_type=F32)


def kernel(
    factor,
    tok_hbm, att_hbm, w_hbm, cot_hbm,
    mixed, gatt, wg,
    tok, a_own, perm, at, w, cot, part,
    bx, br, bfin, bz, gacc,
    term, xr, xfin, xs, zr, zfin, res, resx,
    lsem, ssem, rsem,
):
    dp, tp = lax.axis_index("dp"), lax.axis_index("tensor")
    x, zh, c = dp // 8, (dp // 2) % 4, dp % 2
    y, zl = tp // 2, tp % 2

    def dev(x_, zh_, c_, y_, zl_):
        return ((x_ * 4 + zh_) * 2 + c_, y_ * 2 + zl_)

    xp, xm = dev((x + 1) % 4, zh, c, y, zl), dev((x + 3) % 4, zh, c, y, zl)
    yp, ym = dev(x, zh, c, (y + 1) % 4, zl), dev(x, zh, c, (y + 3) % 4, zl)
    zp, zm = dev(x, (zh + 1) % 4, c, y, zl), dev(x, (zh + 3) % 4, c, y, zl)
    zo, co = dev(x, zh, c, y, 1 - zl), dev(x, zh, 1 - c, y, zl)

    barrier = pltpu.get_barrier_semaphore()
    for to in (xp, xm, yp, ym, zp, zm, zo, co):
        pl.semaphore_signal(barrier, inc=1, device_id=to, device_id_type=MESH)

    def slot(i, k):
        return (0, 2 + k, 3 - k, 1, 6, 4 + k, 5 - k, 7)[i]

    def block(s):
        return ((y + Y_OFF[s]) % 4) * 2 + (zl + Z_OFF[s]) % 2

    def step_block(i, k):
        yo = (0, 3 - 2 * k, 1 + 2 * k, 0, 2, 3 - 2 * k, 1 + 2 * k, 2)[i]
        return ((y + yo) % 4) * 2 + (zl + (0, 0, 0, 1, 0, 1, 1, 1)[i]) % 2

    count = [0]

    def load(src, dst):
        copy = pltpu.make_async_copy(src, dst, lsem.at[count[0]])
        count[0] += 1
        copy.start()
        return copy

    l_cot = [load(cot_hbm.at[:, pl.ds(H * h, H)], cot.at[0, 1 + h]) for h in range(2)]
    l_att = [load(att_hbm.at[h], a_own.at[:, pl.ds(128 * h, 128)]) for h in range(6)]
    sent = []

    def send(src, dst, to):
        i = len(sent)
        copy = pltpu.make_async_remote_copy(
            src_ref=src, dst_ref=dst, send_sem=ssem.at[i], recv_sem=rsem.at[i],
            device_id=to, device_id_type=MESH,
        )
        copy.start()
        sent.append(copy)
        return copy

    a, cx = {}, {}

    def a_send(src, s, h, to):
        a[s, h] = send(cot.at[src, 1 + h], cot.at[s, 1 + h], to)

    def core_send(i):
        s = slot(i, 1 - c)
        cx[i] = send(cot.at[s, 2 - c], cot.at[s, 3 * (1 - c)], co)

    def make_perm(i, _):
        row = lax.broadcasted_iota(jnp.int32, (48, 128), 0)
        core = (row >= 24).astype(jnp.int32)
        r = row - 24 * core
        want = (r >> 2) * 128 + 8 * i + 4 * core + (r & 3)
        want = want - lax.broadcasted_iota(jnp.int32, (48, 128), 1)
        rows = pl.ds(pl.multiple_of((i % 8) * 48, 16), 48)
        for h in range(6):
            perm[i // 8, rows, pl.ds(128 * h, 128)] = (
                jnp.where(want == 128 * h, 1.0, 0.0).astype(BF16)
            )
        return 0

    lax.fori_loop(0, 16, make_perm, 0)
    gacc[...] = jnp.zeros_like(gacc)
    pl.semaphore_wait(barrier, 8)
    l_cot[0].wait()
    l_cot[1].wait()
    a_send(0, 2, 0, yp)
    a_send(0, 3, 1, ym)
    a[1] = [send(cot.at[0, pl.ds(1, 2)], cot.at[1, pl.ds(1, 2)], zo)]
    core_send(0)
    a_send(0, 2, 1, yp)
    a_send(0, 3, 0, ym)
    l_w = {}

    def load_w(s):
        for h in range(2):
            col = pl.multiple_of(block(s) * E + H * h, 128)
            l_w[s, h] = load(w_hbm.at[:, pl.ds(col, H)], w.at[s, h])

    load_w(7)
    for cp in l_att:
        cp.wait()
    mine = pl.ds(pl.multiple_of(T * (1 - c), T), T)

    a_swap = []
    for i in range(2):
        at[i, :, mine] = nt(perm[i], a_own[...]).astype(BF16)
        a_swap.append(send(at.at[i, :, mine], at.at[i, :, mine], co))
    for s in (4, 5, 0, 1, 6, 3, 2):
        load_w(s)
    l_tok = load(tok_hbm, tok)

    x1, x2, zf, zn, zt, r1 = {}, {}, {}, {}, {}, {}
    xf, xn, xl = (x + 2) % 4, (x + 1) % 4, (x + 3) % 4

    def c_term(i):
        cx[i].wait_recv()
        s = slot(i, c)

        val = nn(at[...].reshape(E, 2 * T), cot[s, pl.ds(2 * c, 2)].reshape(2 * T, H))
        term[i] = val.astype(BF16).reshape(4, 4, 48, H)
        parts = [x_parts(i, u) for u in range(2 if i in SPLIT else 1)]
        for u, (p, q) in enumerate(parts):
            x1[i, u] = [
                send(term.at[i, xf, p], xr.at[i, 0, p], xp),
                send(term.at[i, xf, q], xr.at[i, 1, q], xm),
            ]

    def c_near(i, u=0):
        p, q = x_parts(i, u)
        x1[i, u] += [
            send(term.at[i, xn, q], xfin.at[i, 0, q], xp),
            send(term.at[i, xl, p], xfin.at[i, 1, p], xm),
        ]

    def x_parts(i, u):
        if i not in SPLIT:
            return pl.ds(0, 2), pl.ds(2, 2)
        n_p, n_m, _, _ = z_places(i)
        p, q = (((zh + 2) % 4, n_p), (n_m, zh))[u]
        return pl.ds(p, 1), pl.ds(q, 1)

    def c_relay(i, u=0):
        p, q = x_parts(i, u)
        x1[i, u][0].wait_recv()
        t = term[i, xn, p].astype(F32) + xr[i, 0, p].astype(F32)
        term[i, xn, p] = t.astype(BF16)
        x2[i, u] = [send(term.at[i, xn, p], xfin.at[i, 0, p], xp)]
        x1[i, u][1].wait_recv()
        t = term[i, xl, q].astype(F32) + xr[i, 1, q].astype(F32)
        term[i, xl, q] = t.astype(BF16)
        x2[i, u].append(send(term.at[i, xl, q], xfin.at[i, 1, q], xm))

    def z_places(i):
        way = 1 + 2 * ((i + zl + 1) % 2)
        n_p, n_m = (zh + way) % 4, (zh + 4 - way) % 4
        return n_p, n_m, dev(x, n_p, c, y, zl), dev(x, n_m, c, y, zl)

    def c_xsum(i, u=0):
        for cp in x1[i, u][2:] + x2[i, u]:
            cp.wait_recv()
        _, n_m, to_p, to_m = z_places(i)
        for part_z in x_parts(i, u) if i in SPLIT else (pl.ds(0, 4),):
            t = term[i, x, part_z].astype(F32) + xfin[i, 0, part_z].astype(F32)
            xs[i, part_z] = (t + xfin[i, 1, part_z].astype(F32)).astype(BF16)
        if u == 0:
            zf[i] = send(xs.at[i, (zh + 2) % 4], zr.at[i], to_p)
        if u == 1 or i not in SPLIT:
            zn[i] = send(xs.at[i, n_m], zfin.at[i, 1], to_m)

    def c_zrelay(i):
        n_p, _, to_p, _ = z_places(i)
        zf[i].wait_recv()
        t = xs[i, n_p].astype(F32) + zr[i].astype(F32)
        xs[i, n_p] = t.astype(BF16)
        zt[i] = send(xs.at[i, n_p], zfin.at[i, 0], to_p)

    def put(val, col):
        cols = pl.ds(pl.multiple_of(col, 128), H)
        for h in range(6):
            wg[h, :, cols] = val[4 * h : 4 * h + 4]

    def c_zsum(i):
        zn[i].wait_recv()
        zt[i].wait_recv()
        t = xs[i, zh].astype(F32) + zfin[i, 0].astype(F32) + zfin[i, 1].astype(F32)
        res[i] = (t * factor).reshape(2, 24, H)
        r1[i] = send(res.at[i, 1 - c], resx.at[i], co)
        put(res[i, c], step_block(i, c) * E + H * c)

    def c_out(i):
        r1[i].wait_recv()
        put(resx[i], step_block(i, 1 - c) * E + H * (1 - c))

    def w_ready(s):
        for h in range(2):
            if (s, h) in l_w:
                l_w.pop((s, h)).wait()

    def grad(s):
        w_ready(s)

        def go(b, _):
            cols = pl.ds(pl.multiple_of(b * T, T), T)
            t = nt(cot[s, 1], w[s, 0, cols]) + nt(cot[s, 2], w[s, 1, cols])
            gacc[:, cols] += t
            return 0

        lax.fori_loop(0, 3, go, 0)

    def b_part(s):
        w_ready(s)

        def go(h, _):
            part[s, h] = nn(a_own[...], w[s, h]).astype(BF16)
            return 0

        lax.fori_loop(0, 2, go, 0)

    b1 = {}

    def b_over(h):
        b1["x", h] = send(part.at[7, h], bx.at[h], zo)

    def b_near(h):
        b1["n", h] = [
            send(part.at[5, h], bfin.at[0, 0, h], yp),
            send(part.at[4, h], bfin.at[0, 1, h], ym),
        ]

    def b_beside():
        b1["b"] = [
            send(part.at[3, 1], bfin.at[1, 0, 1], yp),
            send(part.at[2, 0], bfin.at[1, 1, 0], ym),
        ]

    def add_to(s, h, ref):
        part[s, h] = (part[s, h].astype(F32) + ref[h].astype(F32)).astype(BF16)

    def b_far():
        b1["f"] = []
        for h, to in ((0, yp), (1, ym)):
            b1["x", h].wait_recv()
            add_to(6, h, bx)
            b1["f"].append(send(part.at[6, h], br.at[h], to))

    def b_relay():
        b1["r"] = []
        for h, s, to in ((0, 3, yp), (1, 2, ym)):
            b1["f"][h].wait_recv()
            add_to(s, h, br)
            b1["r"].append(send(part.at[s, h], bfin.at[1, h, h], to))

    def b_sum(r, h, rows=slice(None)):
        t = part[1 - r, h, rows].astype(F32) + bfin[r, 0, h, rows].astype(F32)
        return t + bfin[r, 1, h, rows].astype(F32)

    def b_cross(h, k):
        for cp in b1.pop(("n", h), ()):
            cp.wait_recv()
        rows = pl.ds(k * (T // 2), T // 2)
        part[1, h, rows] = b_sum(0, h, rows).astype(BF16)
        b1["c", h, k] = send(part.at[1, h, rows], bz.at[h, rows], zo)

    def b_mix():
        for cp in b1["b"] + b1["r"]:
            cp.wait_recv()
        l_tok.wait()
        for h in range(2):
            b1["c", h, 0].wait_recv()
            b1["c", h, 1].wait_recv()
            t = b_sum(1, h) + bz[h].astype(F32)
            cols = pl.ds(H * h, H)
            mixed[:, cols] = (tok[:, cols].astype(F32) + t).astype(BF16)

    def grad_out():
        for h in range(6):
            gatt[h] = gacc[:, pl.ds(128 * h, 128)].astype(BF16)

    drained = [0]

    def drain(n):
        for cp in sent[drained[0] : n]:
            cp.wait_send()
        drained[0] = max(drained[0], n)

    def arrived(*keys):
        for k in keys:
            for cp in a[k] if k == 1 else [a[k]]:
                cp.wait_recv()

    b_part(7)
    for cp in a_swap:
        cp.wait_recv()
    c_term(0)
    c_near(0)
    b_part(4)
    b_part(5)
    grad(0)
    arrived((2, 0), (3, 1))
    a_send(2, 6, 0, yp)
    a_send(3, 6, 1, ym)
    core_send(1)
    c_relay(0)
    c_term(1)
    c_near(1)
    arrived(1)
    core_send(3)
    b_part(1)
    a_send(1, 4, 0, yp)
    a_send(1, 5, 1, ym)
    b_over(0)
    c_term(3)
    c_near(3)
    c_xsum(0)
    c_relay(1)
    b_part(6)
    b_near(0)
    arrived((6, 0), (6, 1))
    core_send(4)
    b_over(1)
    a_send(1, 4, 1, yp)
    a_send(1, 5, 0, ym)
    arrived((2, 1), (3, 0))
    core_send(2)
    grad(3)
    drain(7)
    c_relay(3)
    c_term(4)
    arrived((4, 0), (5, 1))
    a_send(4, 7, 0, yp)
    a_send(5, 7, 1, ym)
    core_send(5)
    b_part(3)
    drain(14)
    c_near(4)
    c_xsum(1)
    c_term(5)
    b_part(2)
    drain(20)
    c_xsum(3)
    b_cross(0, 1)
    c_relay(4)
    c_term(2)
    b_cross(0, 0)
    grad(1)
    drain(28)
    c_near(5)
    b_near(1)
    c_relay(5)
    c_zrelay(1)
    c_near(2)
    arrived((4, 1), (5, 0))
    core_send(6)
    c_xsum(4)
    drain(40)
    b_part(0)
    c_zrelay(0)
    c_term(6)
    c_relay(2)
    c_zrelay(3)
    arrived((7, 0), (7, 1))
    core_send(7)
    c_zrelay(4)
    c_near(6, 0)
    b_far()
    c_xsum(5)
    drain(56)
    c_term(7)
    c_relay(6, 0)
    b_cross(1, 1)
    b_cross(1, 0)
    c_near(7, 0)
    grad(4)
    drain(66)
    c_relay(6, 1)
    c_xsum(2)
    c_zsum(4)
    c_relay(7, 0)
    b_beside()
    c_zrelay(5)
    c_zsum(3)
    drain(77)
    c_near(6, 1)
    c_relay(7, 1)
    c_xsum(6, 0)
    c_near(7, 1)
    grad(6)
    drain(84)
    c_zsum(1)
    c_xsum(7, 0)
    b_relay()
    c_out(3)
    c_xsum(6, 1)
    c_zrelay(2)
    c_zsum(0)
    drain(91)
    grad(2)
    c_zrelay(6)
    c_zsum(5)
    c_xsum(7, 1)
    c_zrelay(7)
    grad(5)
    c_out(0)
    c_out(4)
    c_zsum(2)
    grad(7)
    c_out(2)
    grad_out()
    c_out(1)
    c_zsum(6)
    drain(97)
    c_out(5)
    c_zsum(7)
    b_mix()
    c_out(6)
    c_out(7)
    drain(len(sent))


N_SEND = 144


def body(tokens, attended, out_weight, cotangent):
    factor = 1.0 / math.sqrt(attended.shape[0] * lax.axis_size("dp"))
    any_spec = pl.BlockSpec(memory_space=pl.ANY)
    vm = pltpu.VMEM
    mixed, gatt, wg = pl.pallas_call(
        functools.partial(kernel, factor),
        out_shape=(
            vm((T, E), BF16),
            vm((6, T, 128), BF16),
            vm((6, 4, 8 * E), F32),
        ),
        in_specs=[any_spec] * 4,
        out_specs=(pl.BlockSpec(memory_space=vm),) * 3,
        scratch_shapes=[
            vm((T, E), BF16),
            vm((T, E), BF16),
            vm((2, H, E), BF16),
            vm((2, H, 2 * T), BF16),
            vm((8, 2, E, H), BF16),
            vm((8, 4, T, H), BF16),
            vm((8, 2, T, H), BF16),
            vm((2, T, H), BF16),
            vm((2, T, H), BF16),
            vm((2, 2, 2, T, H), BF16),
            vm((2, T, H), BF16),
            vm((T, E), F32),
            vm((8, 4, 4, 48, H), BF16),
            vm((8, 2, 4, 48, H), BF16),
            vm((8, 2, 4, 48, H), BF16),
            vm((8, 4, 48, H), BF16),
            vm((8, 48, H), BF16),
            vm((8, 2, 48, H), BF16),
            vm((8, 2, 24, H), F32),
            vm((8, 24, H), F32),
            pltpu.SemaphoreType.DMA((25,)),
            pltpu.SemaphoreType.DMA((N_SEND,)),
            pltpu.SemaphoreType.DMA((N_SEND,)),
        ],
        compiler_params=pltpu.CompilerParams(
            collective_id=0, has_side_effects=True, vmem_limit_bytes=56 * 2**20
        ),
    )(
        tokens,
        jnp.transpose(attended, (1, 0, 2)),
        jnp.transpose(out_weight, (1, 0, 2)).reshape(E, 8 * E),
        cotangent,
    )
    return (
        mixed,
        jnp.transpose(gatt, (1, 0, 2)),
        jnp.transpose(wg, (1, 0, 2)),
    )


def solution(mesh):
    placed = (
        P("dp", "tensor"),
        P("dp", "tensor", None),
        P(None, "tensor", None),
        P("dp", "tensor"),
    )
    return jax.shard_map(
        body,
        mesh=mesh,
        in_specs=placed,
        out_specs=(P("dp", "tensor"), P("dp", "tensor", None), P("dp", "tensor", None)),
        check_vma=False,
    )
```
